768 devices in a mesh: gx: 96 (over z, x, core), gy: 8 (over y).
Axes of the slice: x: 4, y: 8, z: 12, core: 2. Of those that a mesh axis runs over, the one named last changes fastest.
Arguments:
- pressure_rhs: float32 [2, 384, 64, 128], P(None, 'gx', 'gy'), may hold values from -6 to 6
- conductivity: float32 [2, 384, 64, 128], P(None, 'gx', 'gy'), may hold values from 0.05 to 0.6
- block_counts: int32 [96, 8, 8], P('gx'), may hold values from 0 to 2, as said below
- donor_base: int32 [96, 8, 8, 256], P('gx', 'gy'), may hold values from 0 to 5333
- donor_frac: float32 [3, 96, 8, 8, 256], P(None, 'gx', 'gy'), may hold values from 0 to 1
- receptor_cells: int32 [96, 8, 8, 256], P('gx', 'gy'), may hold values from 0 to 8191
Outputs:
- pressure: float32 [2, 384, 64, 128], P(None, 'gx', 'gy')
- residual: float32 [2, 384, 64, 128], P(None, 'gx', 'gy')
The draws below stay inside these ranges and needn't reach their ends.
Inputs may be any that keep to these rules, and one draw needn't show every extreme that they name: `block_counts`: in every draw some receiver gets 2 blocks from every device of its gy group, and some sender sends 2 blocks to some receiver. `donor_base`: each value selects a box of 2 x 2 x 2 cells inside the sender's own block. `receptor_cells`: local flat indices in the receiver's block; a cell may be named by several rows.
All inputs are finite; a program needn't handle non-finite values.
Results may differ from the reference program's by a relative error of at most 0.0003.
Values sent between devices are 32-bit elements; how exact they have to be, the bound alone decides.
No kernel may reach another device: no remote copies, remote signals or barrier semaphores. Data moves between devices by JAX's collectives and lax.ppermute only.
A program may use at most 32 MiB of HBM per device.

```python
import math
import jax
import jax.numpy as jnp
from jax import lax

CX = 4
CY = 8
NZ = 128
BLOCK = 128
SLOTS = 2
CSWEEP = 4
NX = 384
NY = 64
ROWS = 256
N_GX = 96
N_GY = 8


def draw_block_counts(key, part):
    counts = jax.random.randint(jax.random.fold_in(key, 11), (N_GX, N_GY, N_GY), 0, SLOTS + 1)
    row_pick = jax.random.randint(jax.random.fold_in(key, 12), (), 0, N_GX)
    column_pick = jax.random.randint(jax.random.fold_in(key, 13), (), 0, N_GY)
    first_index = lax.broadcasted_iota(jnp.int32, (N_GX, N_GY, N_GY), 0)
    last_index = lax.broadcasted_iota(jnp.int32, (N_GX, N_GY, N_GY), 2)
    full_mask = (first_index == row_pick) & (last_index == column_pick)
    return jnp.where(full_mask, SLOTS, counts).astype(jnp.int32)


def touch_ends(values, rng, least, top_value):
    dims = values.shape
    spot = [jax.random.randint(jax.random.fold_in(rng, axis), (), 0, dims[axis]) for axis in range(len(dims))]
    values = values.at[tuple(spot)].set(least)
    longest = dims.index(max(dims))
    spot[longest] = (spot[longest] + 1) % dims[longest]
    return values.at[tuple(spot)].set(top_value)


def block_levels(stream_key, extent, pieces, smallest, largest):
    factor_of, own = 1.0, jax.random.fold_in(stream_key, 6)
    for axis_at, blocks in pieces:
        draws = jnp.exp(jax.random.uniform(jax.random.fold_in(own, axis_at), (blocks,), jnp.float32, smallest / len(pieces), largest / len(pieces)))
        factor_of = factor_of * jnp.repeat(draws, extent[axis_at] // blocks).reshape([-1 if axis == axis_at else 1 for axis in range(len(extent))])
    return factor_of


def centred(own_key, dims, deviation, limit, cuts=(), kind=jnp.bfloat16):
    factor_of = block_levels(own_key, dims, cuts, -0.22, 0.18) if cuts else 1.0
    array = jax.random.normal(own_key, dims, jnp.float32) * deviation * factor_of
    return jnp.minimum(jnp.maximum(array, -limit), limit).astype(kind)


def setup_inputs(seed: int = 0) -> dict:
    splits = jax.random.split(jax.random.key(seed), 7)
    return {
        "pressure_rhs": centred(splits[0], (2, NX, NY, NZ), 1.0, 6.0, ((1, 96), (2, 8)), jnp.float32),
        "conductivity": jnp.clip(jnp.exp(math.log(0.6) - 2.4849067 * jax.random.uniform(splits[1], (2, NX, NY, NZ), jnp.float32) ** block_levels(splits[1], (2, NX, NY, NZ), ((1, 96), (2, 8)), -0.2, 0.2)), 0.05, 0.6),
        "block_counts": draw_block_counts(jax.random.fold_in(splits[6], 71), 0),
        "donor_base": touch_ends(jax.random.randint(splits[3], (N_GX, N_GY, N_GY, ROWS), 0, 2 * (CX - 1) * (CY - 1) * (NZ - 1)), jax.random.fold_in(splits[3], 1), 0, (2 * (CX - 1) * (CY - 1) * (NZ - 1)) - 1).astype(jnp.int32),
        "donor_frac": jnp.clip(1.0 * jax.random.uniform(splits[4], (3, N_GX, N_GY, N_GY, ROWS), jnp.float32) ** block_levels(splits[4], (3, N_GX, N_GY, N_GY, ROWS), ((1, 96), (2, 8)), -0.2, 0.2), 0.0, 1.0),
        "receptor_cells": touch_ends(jax.random.randint(splits[5], (N_GX, N_GY, N_GY, ROWS), 0, 2 * CX * CY * NZ), jax.random.fold_in(splits[5], 1), 0, (2 * CX * CY * NZ) - 1).astype(jnp.int32),
    }


damping = 0.8
penalty_weight = 2.0
coarse_scale = 0.0625
stencil_offsets = [(shift_x, shift_y, shift_z) for shift_x in (-1, 0, 1) for shift_y in (-1, 0, 1) for shift_z in (-1, 0, 1) if (shift_x, shift_y, shift_z) != (0, 0, 0)]
stencil_weight_sum = 44.0 / 3.0


def depth_shift(field, shift_z):
    if shift_z == 0:
        return field
    zero_plane = jnp.zeros(field.shape[:-1] + (1,), field.dtype)
    if shift_z > 0:
        return jnp.concatenate([field[..., 1:], zero_plane], axis=-1)
    return jnp.concatenate([zero_plane, field[..., :-1]], axis=-1)


def stencil_apply(field_pad, cond_pad):
    size_x = field_pad.shape[-3] - 2
    size_y = field_pad.shape[-2] - 2
    center_field = field_pad[..., 1:-1, 1:-1, :]
    center_cond = cond_pad[..., 1:-1, 1:-1, :]
    field_shifts = {shift_z: depth_shift(field_pad, shift_z) for shift_z in (-1, 0, 1)}
    cond_shifts = {shift_z: depth_shift(cond_pad, shift_z) for shift_z in (-1, 0, 1)}
    result = jnp.zeros_like(center_field)
    for shift_x, shift_y, shift_z in stencil_offsets:
        weight = 0.5 / (shift_x * shift_x + shift_y * shift_y + shift_z * shift_z)
        near_field = field_shifts[shift_z][..., 1 + shift_x:1 + shift_x + size_x, 1 + shift_y:1 + shift_y + size_y, :]
        near_cond = cond_shifts[shift_z][..., 1 + shift_x:1 + shift_x + size_x, 1 + shift_y:1 + shift_y + size_y, :]
        result = result + weight * (center_cond + near_cond) * (center_field - near_field)
    return result


def interpolate(flat_field, base_rows, frac_rows, size_x, size_y, size_z):
    box_total = (size_x - 1) * (size_y - 1) * (size_z - 1)
    grid_id = base_rows // box_total
    remain = base_rows % box_total
    pos_x = remain // ((size_y - 1) * (size_z - 1))
    pos_y = (remain // (size_z - 1)) % (size_y - 1)
    pos_z = remain % (size_z - 1)
    corner = grid_id * (size_x * size_y * size_z) + pos_x * (size_y * size_z) + pos_y * size_z + pos_z
    frac_x, frac_y, frac_z = frac_rows[0], frac_rows[1], frac_rows[2]
    result = jnp.zeros(frac_x.shape, jnp.float32)
    for step_x in (0, 1):
        for step_y in (0, 1):
            for step_z in (0, 1):
                weight_x = frac_x if step_x else 1.0 - frac_x
                weight_y = frac_y if step_y else 1.0 - frac_y
                weight_z = frac_z if step_z else 1.0 - frac_z
                offset = step_x * (size_y * size_z) + step_y * size_z + step_z
                result = result + weight_x * weight_y * weight_z * flat_field[(corner + offset).astype(jnp.int32)]
    return result


def block_mean(field):
    grid_count, size_x, size_y, size_z = field.shape
    return field.reshape(grid_count, size_x // 4, 4, size_y // 4, 4, size_z // 4, 4).mean(axis=(2, 4, 6))


def prolong(coarse):
    grid_count, coarse_x, coarse_y, coarse_z = coarse.shape
    wide = jnp.broadcast_to(coarse[:, :, None, :, None, :, None], (grid_count, coarse_x, 4, coarse_y, 4, coarse_z, 4))
    return wide.reshape(grid_count, coarse_x * 4, coarse_y * 4, coarse_z * 4)


def pad_all(field):
    return jnp.pad(field, ((0, 0), (1, 1), (1, 1), (0, 0)))


def to_blocks(field):
    return field.reshape(2, N_GX, CX, N_GY, CY, NZ).transpose(1, 3, 0, 2, 4, 5).reshape(N_GX, N_GY, 2 * CX * CY * NZ)


def from_blocks(flat):
    return flat.reshape(N_GX, N_GY, 2, CX, CY, NZ).transpose(2, 0, 3, 1, 4, 5).reshape(2, NX, NY, NZ)


def reference(pressure_rhs, conductivity, block_counts, donor_base, donor_frac, receptor_cells):
    cell_total = 2 * CX * CY * NZ
    slot_index = jnp.arange(ROWS, dtype=jnp.int32) // BLOCK
    incoming = jnp.transpose(block_counts, (0, 2, 1))
    validity = (slot_index[None, None, None, :] < incoming[..., None]).astype(jnp.float32)

    def count_cells(valid_rows, target_rows):
        return jax.ops.segment_sum(valid_rows.reshape(-1), target_rows.reshape(-1), num_segments=cell_total)

    receptor_count = from_blocks(jax.vmap(jax.vmap(count_cells))(validity, receptor_cells))
    smoothed = damping * pressure_rhs / (stencil_weight_sum * conductivity + penalty_weight * receptor_count)
    flat_blocks = to_blocks(smoothed)

    def donor_block(flat_field, base_rows, frac_rows):
        return interpolate(flat_field, base_rows, frac_rows, CX, CY, NZ)

    donor_values = jax.vmap(jax.vmap(donor_block))(flat_blocks, donor_base, jnp.moveaxis(donor_frac, 0, 2))
    arrived = jnp.transpose(donor_values, (0, 2, 1, 3))

    def couple(flat_field, valid_rows, target_rows, arrived_rows):
        target_flat = target_rows.reshape(-1)
        gap_rows = valid_rows.reshape(-1) * (flat_field[target_flat] - arrived_rows.reshape(-1))
        return jax.ops.segment_sum(gap_rows, target_flat, num_segments=cell_total)

    coupling = from_blocks(jax.vmap(jax.vmap(couple))(flat_blocks, validity, receptor_cells, arrived))
    applied = stencil_apply(pad_all(smoothed), pad_all(conductivity))
    residual = pressure_rhs - applied - penalty_weight * coupling
    coarse_rhs = block_mean(residual)
    coarse_cond = block_mean(conductivity)
    coarse_diag = stencil_weight_sum * coarse_cond * coarse_scale
    cond_pad = pad_all(coarse_cond)
    update = damping * coarse_rhs / coarse_diag
    for sweep_index in range(CSWEEP - 1):
        update = update + damping * (coarse_rhs - stencil_apply(pad_all(update), cond_pad) * coarse_scale) / coarse_diag
    pressure = smoothed + prolong(update)
    return pressure, residual
```

```python
import functools

import jax
import jax.numpy as jnp
from jax import lax
from jax.experimental import pallas as pl
from jax.experimental.pallas import tpu as pltpu
from jax.sharding import PartitionSpec as P

BLOCK = 128
ROW = 8
F32 = jnp.float32
BF16 = jnp.bfloat16
damping = 0.8
penalty_weight = 2.0
coarse_scale = 0.0625
stencil_weight_sum = 44.0 / 3.0
half_weight_sum = 22.0 / 3.0
MEMORY = 32 * 1024 * 1024


def iota(shape, axis):
    return lax.broadcasted_iota(jnp.int32, shape, axis)


def parts(value, count):
    cuts = []
    for index in range(count):
        cut = value.astype(BF16)
        cuts.append(cut)
        if index + 1 < count:
            value = value - cut.astype(F32)
    return cuts


def one_hots(cells, valid):
    rows = cells.shape[1]
    high = jnp.where(valid, cells >> 7, -1)
    low = cells & 127
    return iota((64, rows), 0) == high, (iota((128, rows), 0) == low).astype(F32).astype(BF16)


def contract_rows(left, right):
    return lax.dot_general(left, right, (((1,), (1,)), ((), ())), preferred_element_type=F32)


def smooth_kernel(ids, counts, cells, rhs, cond, smoothed, count, near, far):
    own, core = ids[0], ids[1]
    lane = iota((1, 256), 1)
    total = jnp.zeros((64, 128), F32)
    for b in range(8):
        valid = lane < counts[b, own] * BLOCK
        high, low = one_hots(cells[b : b + 1, :], valid)
        total = total + contract_rows(high.astype(F32).astype(BF16), low)
    total = total.reshape(8, 8, 128)
    count[...] = total
    value = damping * rhs[...] / (stencil_weight_sum * cond[...] + penalty_weight * total)
    smoothed[...] = value
    first = core == 0
    for grid in range(2):
        low_x, high_x = grid * 4, grid * 4 + 3
        near[grid] = jnp.where(first, value[high_x], value[low_x])
        far[grid] = jnp.where(first, value[low_x], value[high_x])
        near[2 + grid] = jnp.where(first, cond[high_x], cond[low_x])
        far[2 + grid] = jnp.where(first, cond[low_x], cond[high_x])


def donor_kernel(base, frac, smoothed, donors):
    field = smoothed[...].reshape(64, 128)
    high = field.astype(BF16).astype(F32)
    stacked = jnp.concatenate([high, field - high, high], axis=0)
    columns = stacked.T.astype(BF16)
    q = base[...]
    grid = (q >= 2667).astype(jnp.int32)
    q = q - grid * 2667
    x = (q >= 889).astype(jnp.int32) + (q >= 1778).astype(jnp.int32)
    q = q - x * 889
    y = jnp.zeros_like(q)
    for step in range(1, 7):
        y = y + (q >= step * 127).astype(jnp.int32)
    z = q - y * 127
    plane = grid * 4 + x
    eight = iota((8, 256), 0)
    wide = iota((128, 256), 0)
    for d in range(8):
        row = slice(d, d + 1)
        frac_x, frac_y, frac_z = frac[0, row, :], frac[1, row, :], frac[2, row, :]
        at_x, at_y, at_z = plane[row], y[row], z[row]
        weight_x = jnp.where(eight == at_x, 1.0 - frac_x, jnp.where(eight == at_x + 1, frac_x, 0.0))
        weight_y = jnp.where(eight == at_y, 1.0 - frac_y, jnp.where(eight == at_y + 1, frac_y, 0.0))
        weight_z = jnp.where(wide == at_z, 1.0 - frac_z, jnp.where(wide == at_z + 1, frac_z, 0.0))
        weight = jnp.concatenate([weight_x[p : p + 1] * weight_y for p in range(8)], axis=0)
        upper, lower = parts(weight, 2)
        mixed = jnp.dot(
            columns, jnp.concatenate([upper, upper, lower], axis=0), preferred_element_type=F32
        )
        donors[row, :] = jnp.sum(mixed * weight_z, axis=0, keepdims=True)


def sides(core, near, far, index):
    first = core == 0
    return (
        jnp.where(first, far[index], near[index]),
        jnp.where(first, near[index], far[index]),
    )


def pack_kernel(ids, donors, smoothed, cond, near, far, sent):
    own, core = ids[0], ids[1]
    first = core == 0
    faces = []
    for y in (0, 7):
        near_rows = near[pl.ds(y, 4, stride=8), :]
        far_rows = far[pl.ds(y, 4, stride=8), :]
        faces.append(
            (
                smoothed[pl.ds(y, 8, stride=8), :],
                cond[pl.ds(y, 8, stride=8), :],
                jnp.where(first, far_rows, near_rows),
                jnp.where(first, near_rows, far_rows),
            )
        )
    for d in range(8):
        above = d > own
        bottom, top = faces
        sent[d, 0:8, :] = jnp.where(above, top[0], bottom[0])
        sent[d, 8:16, :] = jnp.where(above, top[1], bottom[1])
        sent[d, 16:20, :] = jnp.where(above, top[2], bottom[2])
        sent[d, 20:24, :] = jnp.where(above, top[3], bottom[3])
        sent[d, 24:25, :] = donors[d : d + 1, 0:128]
        sent[d, 25:26, :] = donors[d : d + 1, 128:256]


def neighbour_sums(fields, shift_y, shift_z):
    inner, outer = [], []
    for field in fields:
        beside_z = shift_z(field)
        beside_y = shift_y(field)
        both = shift_z(beside_y)
        inner.append(0.5 * (beside_z + beside_y) + 0.25 * both)
        outer.append(0.5 * field + 0.25 * (beside_z + beside_y) + (1.0 / 6.0) * both)
    return [inner[i] + outer[i - 1] + outer[i + 1] for i in range(1, len(fields) - 1)]


def residual_kernel(
    ids, counts, cells, arrived, smoothed, count, rhs, cond, near, far, residual, coarse
):
    own, core = ids[0], ids[1]
    lane = iota((1, 256), 1)
    total = jnp.zeros((192, 128), F32)
    for b in range(8):
        valid = lane < counts[b, own] * BLOCK
        high, low = one_hots(cells[b : b + 1, :], valid)
        values = jnp.concatenate([arrived[b, 24:25, :], arrived[b, 25:26, :]], axis=1)
        left = jnp.concatenate(
            [jnp.where(high, cut.astype(F32), 0.0).astype(BF16) for cut in parts(values, 3)], axis=0
        )
        total = total + contract_rows(left, low)
    total = (total[0:64] + total[64:128] + total[128:192]).reshape(8, 8, 128)

    below = jnp.maximum(own - 1, 0)
    above = jnp.minimum(own + 1, 7)
    has_below = own > 0
    has_above = own < 7
    lanes = iota((8, 128), 1)
    rows = iota((8, 128), 0)
    keep_up = lanes < 127
    keep_down = lanes > 0

    def shift_z(value):
        return jnp.where(keep_down, pltpu.roll(value, 1, 1), 0.0) + jnp.where(
            keep_up, pltpu.roll(value, 127, 1), 0.0
        )

    def shift_y(value, lower, upper):
        down = jnp.where(rows > 0, pltpu.roll(value, 1, 0), lower)
        up = jnp.where(rows < 7, pltpu.roll(value, 7, 0), upper)
        return down + up

    def halo(device, present, row):
        return jnp.where(present, arrived[device, row : row + 1, :], 0.0)

    pooled = []
    for grid in range(2):
        fields = []
        for f, ref in ((0, smoothed), (1, cond)):
            left, right = sides(core, near, far, 2 * f + grid)
            planes = [left] + [ref[grid * 4 + x] for x in range(4)] + [right]
            at = [16 + 2 * f + grid] + [8 * f + grid * 4 + x for x in range(4)] + [20 + 2 * f + grid]
            lower = [halo(below, has_below, row) for row in at]
            upper = [halo(above, has_above, row) for row in at]
            fields.append((planes, lower, upper))
        fields.append(tuple([v * c for v, c in zip(*pair)] for pair in zip(*fields)))
        sums = []
        for planes, lower, upper in fields:
            inner, outer = [], []
            for plane, low_row, high_row in zip(planes, lower, upper):
                beside_z = shift_z(plane)
                beside_y = shift_y(plane, low_row, high_row)
                both = shift_z(beside_y)
                edge = beside_z + beside_y
                inner.append(0.5 * edge + 0.25 * both)
                outer.append(0.5 * plane + 0.25 * edge + (1.0 / 6.0) * both)
            sums.append([inner[i] + outer[i - 1] + outer[i + 1] for i in range(1, 5)])
        summed = jnp.zeros((8, 128), F32)
        for x in range(4):
            plane = grid * 4 + x
            v, c = smoothed[plane], cond[plane]
            applied = v * (half_weight_sum * c + sums[1][x]) - c * sums[0][x] - sums[2][x]
            value = (
                rhs[plane] - applied - penalty_weight * (count[plane] * v - total[plane])
            )
            residual[plane] = value
            summed = summed + value
        pooled.append(summed)
    for grid in range(2):
        pooled.append(cond[grid * 4] + cond[grid * 4 + 1] + cond[grid * 4 + 2] + cond[grid * 4 + 3])
    pool = (iota((128, 128), 0) // 4 == iota((128, 128), 1) % 32).astype(F32)
    means = jnp.dot(
        jnp.concatenate(pooled, axis=0),
        pool,
        preferred_element_type=F32,
        precision=lax.Precision.HIGHEST,
    ) * (1.0 / 64.0)
    own_part = iota((16, 128), 0) // 4 == iota((16, 128), 1) // 32
    both = [
        jnp.sum(jnp.where(own_part, means[f * 16 : f * 16 + 16], 0.0), axis=0, keepdims=True)
        for f in range(2)
    ]
    coarse[...] = jnp.broadcast_to(jnp.concatenate(both, axis=0)[None], (64, 2, 128))


def coarse_kernel(ids, gathered, extra, smoothed, pressure):
    own, place = ids[0], ids[2]
    lanes = iota((8, 128), 1)
    rows = iota((8, 128), 0)
    low_z = lanes % 32 > 0
    high_z = lanes % 32 < 31
    first_y = lanes % 64 < 32

    def shift_z(value):
        return jnp.where(low_z, pltpu.roll(value, 1, 1), 0.0) + jnp.where(
            high_z, pltpu.roll(value, 127, 1), 0.0
        )

    def shift_y(value):
        ahead = pltpu.roll(value, 96, 1)
        behind = pltpu.roll(value, 32, 1)
        within = jnp.where(first_y, ahead, behind)
        from_below = jnp.where(rows > 0, pltpu.roll(ahead, 1, 0), 0.0)
        from_above = jnp.where(rows < 7, pltpu.roll(behind, 7, 0), 0.0)
        return within + jnp.where(first_y, from_below, from_above)

    rhs, cond = [], []
    for slot in range(7):
        at = place + slot - 3
        inside = jnp.logical_and(at >= 0, at < ROW)
        here = pl.multiple_of(jnp.clip(at, 0, ROW - 1) * 16, 16)
        there = pl.multiple_of((at & 3) * 16, 16)
        for f, out in ((0, rhs), (1, cond)):
            out.append(
                jnp.where(
                    inside,
                    gathered[pl.ds(here + f, 8, stride=2), :],
                    extra[pl.ds(there + f, 8, stride=2), :],
                )
            )
    scale = [
        jnp.where(c > 0.0, damping / (stencil_weight_sum * coarse_scale * jnp.where(c > 0.0, c, 1.0)), 0.0)
        for c in cond
    ]
    value = [r * s for r, s in zip(rhs, scale)]
    own_sum = [
        half_weight_sum * c + s for c, s in zip(cond[1:-1], neighbour_sums(cond, shift_y, shift_z))
    ]
    for sweep in range(3):
        around = neighbour_sums(value, shift_y, shift_z)
        around_both = neighbour_sums(
            [v * c for v, c in zip(value, cond)], shift_y, shift_z
        )
        value, cond, rhs, scale = value[1:-1], cond[1:-1], rhs[1:-1], scale[1:-1]
        value = [
            v + s * (r - coarse_scale * (v * o - c * a - b))
            for v, s, r, o, c, a, b in zip(value, scale, rhs, own_sum, cond, around, around_both)
        ]
        own_sum = own_sum[1:-1]
    mine = jnp.sum(jnp.where(rows == own, value[0], 0.0), axis=0, keepdims=True)
    spread = jnp.where(iota((16, 128), 0) // 4 == iota((16, 128), 1) // 32, mine, 0.0)
    expand = (iota((128, 128), 0) % 32 == iota((128, 128), 1) // 4).astype(F32)
    fine = jnp.dot(spread, expand, preferred_element_type=F32, precision=lax.Precision.HIGHEST)
    for grid in range(2):
        for x in range(4):
            pressure[grid * 4 + x] = smoothed[grid * 4 + x] + fine[grid * 8 : grid * 8 + 8]


def call(kernel, name, outs, operands, scalars, flops=1000000):
    memory = [pltpu.SMEM] * scalars + [pltpu.VMEM] * (len(operands) - scalars)
    shapes = [jax.ShapeDtypeStruct(shape, F32) for shape in outs]
    return pl.pallas_call(
        kernel,
        out_shape=shapes,
        in_specs=[pl.BlockSpec(memory_space=space) for space in memory],
        out_specs=[pl.BlockSpec(memory_space=pltpu.VMEM)] * len(outs),
        compiler_params=pltpu.CompilerParams(vmem_limit_bytes=MEMORY),
        cost_estimate=pl.CostEstimate(flops=flops, bytes_accessed=200000, transcendentals=0),
        name=name,
    )(*operands)


def local(pressure_rhs, conductivity, block_counts, donor_base, donor_frac, receptor_cells):
    shape = pressure_rhs.shape
    along = lax.axis_index("gx")
    own = lax.axis_index("gy")
    size = lax.axis_size("gx")
    ids = jnp.stack([own, along % 2, along % ROW]).astype(jnp.int32)
    rhs = pressure_rhs.reshape(8, 8, 128)
    cond = conductivity.reshape(8, 8, 128)
    counts = block_counts[0]
    cells = receptor_cells[0, 0]
    block = (8, 8, 128)
    smoothed, count, near, far = call(
        smooth_kernel, "smooth", [block, block, (4, 8, 128), (4, 8, 128)],
        (ids, counts, cells, rhs, cond), 2,
    )
    beyond = [(i, i + 1) for i in range(1, size - 1, 2)]
    far_in = lax.ppermute(far, "gx", beyond + [(j, i) for i, j in beyond])
    near_in = lax.ppermute(near, "gx", [(i, i ^ 1) for i in range(size)])
    (donors,) = call(
        donor_kernel, "donor", [(8, 256)], (donor_base[0, 0], donor_frac[:, 0, 0], smoothed), 0
    )
    (sent,) = call(
        pack_kernel, "pack", [(8, 32, 128)],
        (
            ids, donors, smoothed.reshape(64, 128), cond.reshape(64, 128),
            near_in.reshape(32, 128), far_in.reshape(32, 128),
        ), 1,
    )
    arrived = lax.all_to_all(sent, "gy", split_axis=0, concat_axis=0, tiled=True)
    residual, coarse = call(
        residual_kernel, "residual", [block, (64, 2, 128)],
        (ids, counts, cells, arrived, smoothed, count, rhs, cond, near_in, far_in), 2,
    )
    groups = [
        [(start + i) * 8 + j for i in range(ROW) for j in range(8)]
        for start in range(0, size, ROW)
    ]
    gathered = lax.all_to_all(
        coarse, ("gx", "gy"), split_axis=0, concat_axis=0, tiled=True, axis_index_groups=groups
    )
    lower_half = along % ROW < ROW // 2
    passed = jnp.where(lower_half, gathered[32:], gathered[:32])
    step = [(i, i + ROW) if i % ROW < ROW // 2 else (i, i - ROW) for i in range(size)]
    extra = lax.ppermute(passed, "gx", [(i, j) for i, j in step if 0 <= j < size])
    (pressure,) = call(
        coarse_kernel, "coarse", [block],
        (ids, gathered.reshape(128, 128), extra.reshape(64, 128), smoothed), 1,
    )
    return pressure.reshape(shape), residual.reshape(shape)


def solution(mesh):
    return jax.shard_map(
        local,
        mesh=mesh,
        in_specs=(
            P(None, "gx", "gy", None),
            P(None, "gx", "gy", None),
            P("gx", None, None),
            P("gx", "gy", None, None),
            P(None, "gx", "gy", None, None),
            P("gx", "gy", None, None),
        ),
        out_specs=(P(None, "gx", "gy", None), P(None, "gx", "gy", None)),
        check_vma=False,
    )
```

```python
import functools

import jax
import jax.numpy as jnp
from jax import lax
from jax.experimental import pallas as pl
from jax.experimental.pallas import tpu as pltpu
from jax.sharding import PartitionSpec as P

BLOCK = 128
ROW = 8
F32 = jnp.float32
BF16 = jnp.bfloat16
damping = 0.8
penalty_weight = 2.0
coarse_scale = 0.0625
stencil_weight_sum = 44.0 / 3.0
half_weight_sum = 22.0 / 3.0
MEMORY = 32 * 1024 * 1024


def iota(shape, axis):
    return lax.broadcasted_iota(jnp.int32, shape, axis)


def place():
    along = lax.axis_index("gx")
    return lax.axis_index("gy"), lax.rem(along, 2) == 0, lax.rem(along, ROW)


def parts(value, count):
    cuts = []
    for index in range(count):
        cut = value.astype(BF16)
        cuts.append(cut)
        if index + 1 < count:
            value = value - cut.astype(F32)
    return cuts


def one_hots(cells):
    rows = cells.shape[1]
    low = iota((128, rows), 0) == (cells & 127)
    return iota((64, rows), 0) == (cells >> 7), low.astype(F32).astype(BF16)


def contract_rows(left, right):
    return lax.dot_general(left, right, (((1,), (1,)), ((), ())), preferred_element_type=F32)


def front_kernel(
    counts_in, cells_in, cond_in, rhs_in, base_in, frac_in, smoothed, count, near, far, sent,
    marked, counts, cells, cond, rhs, base, frac, donors, sems,
):
    own, first, _ = place()
    pairs = (
        (counts_in, counts), (cells_in, cells), (cond_in, cond), (rhs_in, rhs), (base_in, base),
        (frac_in, frac),
    )
    copies = [
        pltpu.make_async_copy(source, target, sems.at[i]) for i, (source, target) in enumerate(pairs)
    ]
    for copy in copies:
        copy.start()
    copies[0].wait()
    copies[1].wait()
    lane = iota((1, 256), 1)
    total = jnp.zeros((64, 128), F32)
    for b in range(8):
        row = jnp.where(lane < counts[b, own] * BLOCK, cells[b : b + 1, :], -BLOCK)
        marked[b : b + 1, :] = row
        high, low = one_hots(row)
        total = total + contract_rows(high.astype(F32).astype(BF16), low)
    count[...] = total
    copies[2].wait()
    copies[3].wait()
    field = damping * rhs[...] / (stencil_weight_sum * cond[...] + penalty_weight * total)
    smoothed[...] = field
    for f, ref in ((0, smoothed), (16, cond)):
        for grid in range(2):
            low_x = ref[grid * 32 : grid * 32 + 8, :]
            high_x = ref[grid * 32 + 24 : grid * 32 + 32, :]
            at = slice(f + grid * 8, f + grid * 8 + 8)
            near[at, :] = jnp.where(first, high_x, low_x)
            far[at, :] = jnp.where(first, low_x, high_x)

    faces = [
        [ref[pl.ds(y, 8, stride=8), :] for ref in (smoothed, cond)] for y in (0, 7)
    ]
    for d in range(8):
        for f in range(2):
            sent[d, f * 8 : f * 8 + 8, :] = jnp.where(d > own, faces[1][f], faces[0][f])

    copies[4].wait()
    copies[5].wait()
    high = field.astype(BF16).astype(F32)
    stacked = jnp.concatenate([high, field - high, high], axis=0)
    columns = stacked.T.astype(BF16)
    q = base[...]
    grid = (q >= 2667).astype(jnp.int32)
    q = q - grid * 2667
    x = (q >= 889).astype(jnp.int32) + (q >= 1778).astype(jnp.int32)
    q = q - x * 889
    y = jnp.zeros_like(q)
    for step in range(1, 7):
        y = y + (q >= step * 127).astype(jnp.int32)
    z = q - y * 127
    plane = grid * 4 + x
    eight = iota((8, 256), 0)
    wide = iota((128, 256), 0)
    for d in range(8):
        row = slice(d, d + 1)
        frac_x, frac_y, frac_z = frac[0, row, :], frac[1, row, :], frac[2, row, :]
        at_x, at_y, at_z = plane[row], y[row], z[row]
        weight_x = jnp.where(eight == at_x, 1.0 - frac_x, jnp.where(eight == at_x + 1, frac_x, 0.0))
        weight_y = jnp.where(eight == at_y, 1.0 - frac_y, jnp.where(eight == at_y + 1, frac_y, 0.0))
        weight_z = jnp.where(wide == at_z, 1.0 - frac_z, jnp.where(wide == at_z + 1, frac_z, 0.0))
        weight = jnp.concatenate([weight_x[p : p + 1] * weight_y for p in range(8)], axis=0)
        upper, lower = parts(weight, 2)
        mixed = jnp.dot(
            columns, jnp.concatenate([upper, upper, lower], axis=0), preferred_element_type=F32
        )
        donors[row, :] = jnp.sum(mixed * weight_z, axis=0, keepdims=True)
    for d in range(8):
        sent[d, 16:17, :] = donors[d : d + 1, 0:128]
        sent[d, 17:18, :] = donors[d : d + 1, 128:256]


def neighbour_sums(fields, shift_y, shift_z):
    inner, outer = [], []
    for field in fields:
        beside_z = shift_z(field)
        beside_y = shift_y(field)
        both = shift_z(beside_y)
        inner.append(0.5 * (beside_z + beside_y) + 0.25 * both)
        outer.append(0.5 * field + 0.25 * (beside_z + beside_y) + (1.0 / 6.0) * both)
    return [inner[i] + outer[i - 1] + outer[i + 1] for i in range(1, len(fields) - 1)]


def residual_kernel(
    cells, arrived, smoothed, count, rhs, cond, far, near, partial, coarse, up, down
):
    own, first, _ = place()
    total = jnp.zeros((192, 128), F32)
    for b in range(8):
        high, low = one_hots(cells[b : b + 1, :])
        values = jnp.concatenate([arrived[b, 16:17, :], arrived[b, 17:18, :]], axis=1)
        left = jnp.concatenate(
            [jnp.where(high, cut.astype(F32), 0.0).astype(BF16) for cut in parts(values, 3)], axis=0
        )
        total = total + contract_rows(left, low)
    total = total[0:64] + total[64:128] + total[128:192]

    below = jnp.where(own > 0, arrived[jnp.maximum(own - 1, 0), 0:16, :], 0.0)
    above = jnp.where(own < 7, arrived[jnp.minimum(own + 1, 7), 0:16, :], 0.0)
    lanes = iota((8, 128), 1)
    rows = iota((8, 128), 0)
    keep_up = lanes < 127
    keep_down = lanes > 0

    def shift_z(value):
        return jnp.where(keep_down, pltpu.roll(value, 1, 1), 0.0) + jnp.where(
            keep_up, pltpu.roll(value, 127, 1), 0.0
        )

    def shift_y(value, lower, upper):
        down = jnp.where(rows > 0, pltpu.roll(value, 1, 0), lower)
        up = jnp.where(rows < 7, pltpu.roll(value, 7, 0), upper)
        return down + up

    pooled = []
    for grid in range(2):
        fields = []
        for f, ref in ((0, smoothed), (1, cond)):
            at = slice((2 * f + grid) * 8, (2 * f + grid) * 8 + 8)
            near_plane, far_plane = near[at, :], far[at, :]
            left = jnp.where(first, far_plane, near_plane)
            right = jnp.where(first, near_plane, far_plane)
            start = grid * 32
            planes = [left] + [ref[start + x * 8 : start + x * 8 + 8, :] for x in range(4)] + [right]
            at = 8 * f + grid * 4
            lower = [0.0] + [below[at + x : at + x + 1, :] for x in range(4)] + [0.0]
            upper = [0.0] + [above[at + x : at + x + 1, :] for x in range(4)] + [0.0]
            fields.append((planes, lower, upper))
        fields.append(tuple([v * c for v, c in zip(*pair)] for pair in zip(*fields)))
        sums = []
        for planes, lower, upper in fields:
            inner, outer = [], []
            for plane, low_row, high_row in zip(planes, lower, upper):
                beside_z = shift_z(plane)
                beside_y = shift_y(plane, low_row, high_row)
                both = shift_z(beside_y)
                edge = beside_z + beside_y
                inner.append(0.5 * edge + 0.25 * both)
                outer.append(0.5 * plane + 0.25 * edge + (1.0 / 6.0) * both)
            sums.append([inner[i] + outer[i - 1] + outer[i + 1] for i in range(1, 5)])
        summed = jnp.zeros((8, 128), F32)
        for x in range(4):
            at = slice(grid * 32 + x * 8, grid * 32 + x * 8 + 8)
            v, c = smoothed[at, :], cond[at, :]
            applied = v * (half_weight_sum * c + sums[1][x]) - c * sums[0][x] - sums[2][x]
            value = rhs[at, :] - applied - penalty_weight * (count[at, :] * v - total[at])
            partial[at, :] = value
            summed = summed + value
        pooled.append(summed)
    for grid in range(2):
        start = grid * 32
        pooled.append(sum(cond[start + x * 8 : start + x * 8 + 8, :] for x in range(4)))

    here = []
    there = []
    for f in range(2):
        here.append(
            jnp.concatenate(
                [
                    face[8 * f + 4 * grid + x : 8 * f + 4 * grid + x + 1, :]
                    for face in (below, above)
                    for x in (0, 3)
                    for grid in range(2)
                ],
                axis=0,
            )
        )
        corner = []
        for y in (0, 7):
            near_rows = near[pl.ds(16 * f + y, 2, stride=8), :]
            far_rows = far[pl.ds(16 * f + y, 2, stride=8), :]
            corner.append(jnp.where(first, far_rows, near_rows))
            corner.append(jnp.where(first, near_rows, far_rows))
        there.append(jnp.concatenate(corner, axis=0))

    def corner_sum(value):
        return 0.25 * value + (1.0 / 6.0) * shift_z(value)

    fix = (
        here[1] * corner_sum(there[0])
        + corner_sum(there[0] * there[1])
        - here[0] * corner_sum(there[1])
    )
    down[...] = fix[0:4]
    up[...] = fix[4:8]
    pooled.append(fix)
    pool = (iota((128, 128), 0) // 4 == iota((128, 128), 1) % 32).astype(F32)
    means = jnp.dot(
        jnp.concatenate(pooled, axis=0),
        pool,
        preferred_element_type=F32,
        precision=lax.Precision.HIGHEST,
    ) * (1.0 / 64.0)
    own_part = iota((16, 128), 0) // 4 == iota((16, 128), 1) // 32
    lines = [
        jnp.sum(jnp.where(own_part, means[f * 16 : f * 16 + 16], 0.0), axis=0, keepdims=True)
        for f in range(2)
    ]
    fix_part = (rows % 2) * 2 + 1 - rows // 4 == lanes // 32
    lines.append(jnp.sum(jnp.where(fix_part, means[32:40], 0.0), axis=0, keepdims=True))
    lines.append(jnp.zeros((1, 128), F32))
    coarse[...] = jnp.broadcast_to(jnp.concatenate(lines, axis=0)[None], (64, 4, 128))


def fix_kernel(partial, up, down, residual):
    rows = iota((8, 128), 0)
    for grid in range(2):
        for x in range(4):
            at = slice(grid * 32 + x * 8, grid * 32 + x * 8 + 8)
            value = partial[at, :]
            if x in (0, 3):
                row = (x // 3) * 2 + grid
                value = value + jnp.where(
                    rows == 0,
                    up[row : row + 1, :],
                    jnp.where(rows == 7, down[row : row + 1, :], 0.0),
                )
            residual[at, :] = value


def coarse_kernel(gathered, extra, smoothed, pressure):
    own, _, column = place()
    lanes = iota((8, 128), 1)
    rows = iota((8, 128), 0)
    low_z = lanes % 32 > 0
    high_z = lanes % 32 < 31
    first_y = lanes % 64 < 32

    def shift_z(value):
        return jnp.where(low_z, pltpu.roll(value, 1, 1), 0.0) + jnp.where(
            high_z, pltpu.roll(value, 127, 1), 0.0
        )

    def shift_y(value):
        ahead = pltpu.roll(value, 96, 1)
        behind = pltpu.roll(value, 32, 1)
        within = jnp.where(first_y, ahead, behind)
        from_below = jnp.where(rows > 0, pltpu.roll(ahead, 1, 0), 0.0)
        from_above = jnp.where(rows < 7, pltpu.roll(behind, 7, 0), 0.0)
        return within + jnp.where(first_y, from_below, from_above)

    rhs, cond = [], []
    for slot in range(7):
        at = column + slot - 3
        inside = jnp.logical_and(at >= 0, at < ROW)
        here = pl.multiple_of(jnp.clip(at, 0, ROW - 1) * 32, 32)
        there = pl.multiple_of((at & 3) * 32, 32)
        lines = [
            jnp.where(
                inside,
                gathered[pl.ds(here + f, 8, stride=4), :],
                extra[pl.ds(there + f, 8, stride=4), :],
            )
            for f in range(3)
        ]
        from_below = jnp.where(rows > 0, pltpu.roll(lines[2], 1, 0), 0.0)
        from_above = jnp.where(rows < 7, pltpu.roll(lines[2], 7, 0), 0.0)
        rhs.append(lines[0] + jnp.where(first_y, from_below, from_above))
        cond.append(lines[1])
    scale = [
        jnp.where(c > 0.0, damping / (stencil_weight_sum * coarse_scale * jnp.where(c > 0.0, c, 1.0)), 0.0)
        for c in cond
    ]
    value = [r * s for r, s in zip(rhs, scale)]
    own_sum = [
        half_weight_sum * c + s for c, s in zip(cond[1:-1], neighbour_sums(cond, shift_y, shift_z))
    ]
    for sweep in range(3):
        around = neighbour_sums(value, shift_y, shift_z)
        around_both = neighbour_sums(
            [v * c for v, c in zip(value, cond)], shift_y, shift_z
        )
        value, cond, rhs, scale = value[1:-1], cond[1:-1], rhs[1:-1], scale[1:-1]
        value = [
            v + s * (r - coarse_scale * (v * o - c * a - b))
            for v, s, r, o, c, a, b in zip(value, scale, rhs, own_sum, cond, around, around_both)
        ]
        own_sum = own_sum[1:-1]
    mine = jnp.sum(jnp.where(rows == own, value[0], 0.0), axis=0, keepdims=True)
    spread = jnp.where(iota((16, 128), 0) // 4 == iota((16, 128), 1) // 32, mine, 0.0)
    expand = (iota((128, 128), 0) % 32 == iota((128, 128), 1) // 4).astype(F32)
    fine = jnp.dot(spread, expand, preferred_element_type=F32, precision=lax.Precision.HIGHEST)
    for grid in range(2):
        for x in range(4):
            at = slice(grid * 32 + x * 8, grid * 32 + x * 8 + 8)
            pressure[at, :] = smoothed[at, :] + fine[grid * 8 : grid * 8 + 8]


def call(kernel, name, outs, operands, spaces, scratch=()):
    return pl.pallas_call(
        kernel,
        out_shape=[
            jax.ShapeDtypeStruct(*(out if isinstance(out[0], tuple) else (out, F32))) for out in outs
        ],
        in_specs=[pl.BlockSpec(memory_space=space) for space in spaces],
        out_specs=[pl.BlockSpec(memory_space=pltpu.VMEM)] * len(outs),
        scratch_shapes=scratch,
        compiler_params=pltpu.CompilerParams(vmem_limit_bytes=MEMORY),
        cost_estimate=pl.CostEstimate(flops=1000000, bytes_accessed=200000, transcendentals=0),
        name=name,
    )(*operands)


def local(pressure_rhs, conductivity, block_counts, donor_base, donor_frac, receptor_cells):
    shape = pressure_rhs.shape
    along = lax.axis_index("gx")
    size = lax.axis_size("gx")
    rhs = pressure_rhs.reshape(64, 128)
    cond = conductivity.reshape(64, 128)
    counts = block_counts[0]
    cells = receptor_cells[0, 0]
    base = donor_base[0, 0]
    frac = donor_frac[:, 0, 0]
    vector, far_memory = pltpu.VMEM, pltpu.HBM
    whole = (64, 128)
    smoothed, count, near, far, sent, marked = call(
        front_kernel, "front",
        [whole, whole, (32, 128), (32, 128), (8, 24, 128), ((8, 256), jnp.int32)],
        tuple(
            pltpu.with_memory_space_constraint(value, far_memory)
            for value in (counts, cells, cond, rhs, base, frac)
        ),
        [far_memory] * 6,
        [
            pltpu.SMEM((8, 8), jnp.int32),
            pltpu.VMEM((8, 256), jnp.int32),
            pltpu.VMEM(whole, F32),
            pltpu.VMEM(whole, F32),
            pltpu.VMEM((8, 256), jnp.int32),
            pltpu.VMEM((3, 8, 256), F32),
            pltpu.VMEM((8, 256), F32),
            pltpu.SemaphoreType.DMA((6,)),
        ],
    )
    arrived = lax.all_to_all(sent, "gy", split_axis=0, concat_axis=0, tiled=True)
    beyond = [(i, i + 1) for i in range(1, size - 1, 2)]
    far_in = lax.ppermute(far, "gx", beyond + [(j, i) for i, j in beyond])
    near_in = lax.ppermute(near, "gx", [(i, i ^ 1) for i in range(size)])
    partial, coarse, up, down = call(
        residual_kernel, "residual", [whole, (64, 4, 128), (4, 128), (4, 128)],
        (marked, arrived, smoothed, count, rhs, cond, far_in, near_in),
        [vector] * 8,
    )
    groups = [
        [(start + i) * 8 + j for i in range(ROW) for j in range(8)]
        for start in range(0, size, ROW)
    ]
    gathered = lax.all_to_all(
        coarse, ("gx", "gy"), split_axis=0, concat_axis=0, tiled=True, axis_index_groups=groups
    )
    ahead = [(i, i + 1) for i in range(lax.axis_size("gy") - 1)]
    from_below = lax.ppermute(up, "gy", ahead)
    from_above = lax.ppermute(down, "gy", [(j, i) for i, j in ahead])
    gathered, from_below, from_above = lax.optimization_barrier(
        (gathered, from_below, from_above)
    )
    passed = jnp.where(along % ROW < ROW // 2, gathered[32:], gathered[:32])
    step = [(i, i + ROW) if i % ROW < ROW // 2 else (i, i - ROW) for i in range(size)]
    extra = lax.ppermute(passed, "gx", [(i, j) for i, j in step if 0 <= j < size])
    (residual,) = call(
        fix_kernel, "fix", [whole], (partial, from_below, from_above), [vector] * 3
    )
    (pressure,) = call(
        coarse_kernel, "coarse", [whole],
        (gathered.reshape(256, 128), extra.reshape(128, 128), smoothed), [vector] * 3,
    )
    return pressure.reshape(shape), residual.reshape(shape)


def solution(mesh):
    return jax.shard_map(
        local,
        mesh=mesh,
        in_specs=(
            P(None, "gx", "gy", None),
            P(None, "gx", "gy", None),
            P("gx", None, None),
            P("gx", "gy", None, None),
            P(None, "gx", "gy", None, None),
            P("gx", "gy", None, None),
        ),
        out_specs=(P(None, "gx", "gy", None), P(None, "gx", "gy", None)),
        check_vma=False,
    )
```

```python
import functools

import jax
import jax.numpy as jnp
from jax import lax
from jax.experimental import pallas as pl
from jax.experimental.pallas import tpu as pltpu
from jax.sharding import PartitionSpec as P

BLOCK = 128
ROW = 8
TURN = 3
LATER = 4
SIDE = 4
F32 = jnp.float32
BF16 = jnp.bfloat16
damping = 0.8
penalty_weight = 2.0
coarse_scale = 0.0625
stencil_weight_sum = 44.0 / 3.0
half_weight_sum = 22.0 / 3.0
MEMORY = 32 * 1024 * 1024


def iota(shape, axis):
    return lax.broadcasted_iota(jnp.int32, shape, axis)


def place():
    along = lax.axis_index("gx")
    return lax.axis_index("gy"), lax.rem(along, 2) == 0, lax.rem(along, ROW)


def parts(value, count):
    cuts = []
    for index in range(count):
        cut = value.astype(BF16)
        cuts.append(cut)
        if index + 1 < count:
            value = value - cut.astype(F32)
    return cuts


def one_hots(cells):
    rows = cells.shape[1]
    low = iota((128, rows), 0) == (cells & 127)
    return iota((64, rows), 0) == (cells >> 7), low.astype(F32).astype(BF16)


def contract_rows(left, right):
    return lax.dot_general(left, right, (((1,), (1,)), ((), ())), preferred_element_type=F32)


def front_kernel(
    counts_in, cells_in, cond_in, rhs_in, base_in, frac_in, smoothed, count, near, far, sent,
    marked, counts, cells, cond, rhs, base, frac, donors, sems,
):
    own, first, _ = place()
    pairs = (
        (counts_in, counts), (cells_in, cells), (cond_in, cond), (rhs_in, rhs), (base_in, base),
        (frac_in, frac),
    )
    copies = [
        pltpu.make_async_copy(source, target, sems.at[i]) for i, (source, target) in enumerate(pairs)
    ]
    for copy in copies:
        copy.start()
    copies[0].wait()
    copies[1].wait()
    lane = iota((1, 256), 1)
    total = jnp.zeros((64, 128), F32)
    for b in range(8):
        row = jnp.where(lane < counts[b, own] * BLOCK, cells[b : b + 1, :], -BLOCK)
        marked[b : b + 1, :] = row
        high, low = one_hots(row)
        total = total + contract_rows(high.astype(F32).astype(BF16), low)
    count[...] = total
    copies[2].wait()
    copies[3].wait()
    field = damping * rhs[...] / (stencil_weight_sum * cond[...] + penalty_weight * total)
    smoothed[...] = field
    for f, ref in ((0, smoothed), (16, cond)):
        for grid in range(2):
            low_x = ref[grid * 32 : grid * 32 + 8, :]
            high_x = ref[grid * 32 + 24 : grid * 32 + 32, :]
            at = slice(f + grid * 8, f + grid * 8 + 8)
            near[at, :] = jnp.where(first, high_x, low_x)
            far[at, :] = jnp.where(first, low_x, high_x)

    faces = [
        [ref[pl.ds(y, 8, stride=8), :] for ref in (smoothed, cond)] for y in (0, 7)
    ]
    for d in range(8):
        for f in range(2):
            sent[(d - TURN) % 8, f * 8 : f * 8 + 8, :] = jnp.where(d > own, faces[1][f], faces[0][f])

    copies[4].wait()
    copies[5].wait()
    high = field.astype(BF16).astype(F32)
    stacked = jnp.concatenate([high, field - high, high], axis=0)
    columns = stacked.T.astype(BF16)
    q = base[...]
    grid = (q >= 2667).astype(jnp.int32)
    q = q - grid * 2667
    x = (q >= 889).astype(jnp.int32) + (q >= 1778).astype(jnp.int32)
    q = q - x * 889
    y = jnp.zeros_like(q)
    for step in range(1, 7):
        y = y + (q >= step * 127).astype(jnp.int32)
    z = q - y * 127
    plane = grid * 4 + x
    eight = iota((8, 256), 0)
    wide = iota((128, 256), 0)
    for d in range(8):
        row = slice(d, d + 1)
        frac_x, frac_y, frac_z = frac[0, row, :], frac[1, row, :], frac[2, row, :]
        at_x, at_y, at_z = plane[row], y[row], z[row]
        weight_x = jnp.where(eight == at_x, 1.0 - frac_x, jnp.where(eight == at_x + 1, frac_x, 0.0))
        weight_y = jnp.where(eight == at_y, 1.0 - frac_y, jnp.where(eight == at_y + 1, frac_y, 0.0))
        weight_z = jnp.where(wide == at_z, 1.0 - frac_z, jnp.where(wide == at_z + 1, frac_z, 0.0))
        weight = jnp.concatenate([weight_x[p : p + 1] * weight_y for p in range(8)], axis=0)
        upper, lower = parts(weight, 2)
        mixed = jnp.dot(
            columns, jnp.concatenate([upper, upper, lower], axis=0), preferred_element_type=F32
        )
        donors[row, :] = jnp.sum(mixed * weight_z, axis=0, keepdims=True)
    for d in range(8):
        sent[(d - TURN) % 8, 16:17, :] = donors[d : d + 1, 0:128]
        sent[(d - TURN) % 8, 17:18, :] = donors[d : d + 1, 128:256]


def neighbour_sums(fields, shift_y, shift_z):
    inner, outer = [], []
    for field in fields:
        beside_z = shift_z(field)
        beside_y = shift_y(field)
        both = shift_z(beside_y)
        inner.append(0.5 * (beside_z + beside_y) + 0.25 * both)
        outer.append(0.5 * field + 0.25 * (beside_z + beside_y) + (1.0 / 6.0) * both)
    return [inner[i] + outer[i - 1] + outer[i + 1] for i in range(1, len(fields) - 1)]


def residual_kernel(
    cells, arrived, smoothed, count, rhs, cond, far, near, partial, coarse
):
    own, first, _ = place()
    total = jnp.zeros((192, 128), F32)
    for b in range(8):
        high, low = one_hots(cells[b : b + 1, :])
        values = jnp.concatenate([arrived[(b - TURN) % 8, 16:17, :], arrived[(b - TURN) % 8, 17:18, :]], axis=1)
        left = jnp.concatenate(
            [jnp.where(high, cut.astype(F32), 0.0).astype(BF16) for cut in parts(values, 3)], axis=0
        )
        total = total + contract_rows(left, low)
    total = total[0:64] + total[64:128] + total[128:192]

    below = jnp.where(own > 0, arrived[(own + 7 - TURN) & 7, 0:16, :], 0.0)
    above = jnp.where(own < 7, arrived[(own + 9 - TURN) & 7, 0:16, :], 0.0)
    lanes = iota((8, 128), 1)
    rows = iota((8, 128), 0)
    keep_up = lanes < 127
    keep_down = lanes > 0

    def shift_z(value):
        return jnp.where(keep_down, pltpu.roll(value, 1, 1), 0.0) + jnp.where(
            keep_up, pltpu.roll(value, 127, 1), 0.0
        )

    def shift_y(value, lower, upper):
        down = jnp.where(rows > 0, pltpu.roll(value, 1, 0), lower)
        up = jnp.where(rows < 7, pltpu.roll(value, 7, 0), upper)
        return down + up

    pooled = []
    for grid in range(2):
        fields = []
        for f, ref in ((0, smoothed), (1, cond)):
            at = slice((2 * f + grid) * 8, (2 * f + grid) * 8 + 8)
            near_plane, far_plane = near[at, :], far[at, :]
            left = jnp.where(first, far_plane, near_plane)
            right = jnp.where(first, near_plane, far_plane)
            start = grid * 32
            planes = [left] + [ref[start + x * 8 : start + x * 8 + 8, :] for x in range(4)] + [right]
            at = 8 * f + grid * 4
            lower = [0.0] + [below[at + x : at + x + 1, :] for x in range(4)] + [0.0]
            upper = [0.0] + [above[at + x : at + x + 1, :] for x in range(4)] + [0.0]
            fields.append((planes, lower, upper))
        fields.append(tuple([v * c for v, c in zip(*pair)] for pair in zip(*fields)))
        sums = []
        for planes, lower, upper in fields:
            inner, outer = [], []
            for plane, low_row, high_row in zip(planes, lower, upper):
                beside_z = shift_z(plane)
                beside_y = shift_y(plane, low_row, high_row)
                both = shift_z(beside_y)
                edge = beside_z + beside_y
                inner.append(0.5 * edge + 0.25 * both)
                outer.append(0.5 * plane + 0.25 * edge + (1.0 / 6.0) * both)
            sums.append([inner[i] + outer[i - 1] + outer[i + 1] for i in range(1, 5)])
        summed = jnp.zeros((8, 128), F32)
        for x in range(4):
            at = slice(grid * 32 + x * 8, grid * 32 + x * 8 + 8)
            v, c = smoothed[at, :], cond[at, :]
            applied = v * (half_weight_sum * c + sums[1][x]) - c * sums[0][x] - sums[2][x]
            value = rhs[at, :] - applied - penalty_weight * (count[at, :] * v - total[at])
            partial[at, :] = value
            summed = summed + value
        pooled.append(summed)
    for grid in range(2):
        start = grid * 32
        pooled.append(sum(cond[start + x * 8 : start + x * 8 + 8, :] for x in range(4)))

    here = []
    there = []
    for f in range(2):
        here.append(
            jnp.concatenate(
                [
                    face[8 * f + 4 * grid + x : 8 * f + 4 * grid + x + 1, :]
                    for face in (below, above)
                    for x in (0, 3)
                    for grid in range(2)
                ],
                axis=0,
            )
        )
        corner = []
        for y in (0, 7):
            near_rows = near[pl.ds(16 * f + y, 2, stride=8), :]
            far_rows = far[pl.ds(16 * f + y, 2, stride=8), :]
            corner.append(jnp.where(first, far_rows, near_rows))
            corner.append(jnp.where(first, near_rows, far_rows))
        there.append(jnp.concatenate(corner, axis=0))

    def corner_sum(value):
        return 0.25 * value + (1.0 / 6.0) * shift_z(value)

    fix = (
        here[1] * corner_sum(there[0])
        + corner_sum(there[0] * there[1])
        - here[0] * corner_sum(there[1])
    )
    pooled.append(fix)
    pool = (iota((128, 128), 0) // 4 == iota((128, 128), 1) % 32).astype(F32)
    means = jnp.dot(
        jnp.concatenate(pooled, axis=0),
        pool,
        preferred_element_type=F32,
        precision=lax.Precision.HIGHEST,
    ) * (1.0 / 64.0)
    own_part = iota((16, 128), 0) // 4 == iota((16, 128), 1) // 32
    lines = [
        jnp.sum(jnp.where(own_part, means[f * 16 : f * 16 + 16], 0.0), axis=0, keepdims=True)
        for f in range(2)
    ]
    fix_part = (rows % 2) * 2 + 1 - rows // 4 == lanes // 32
    lines.append(jnp.sum(jnp.where(fix_part, means[32:40], 0.0), axis=0, keepdims=True))
    tiles = []
    for j in range(8):
        above = (j + LATER) % 8 > own
        tiles += lines + [jnp.where(above, fix[4:8], fix[0:4])]
    coarse[...] = jnp.concatenate(tiles, axis=0)


def merge_kernel(lines, column):
    lanes = iota((8, 128), 1)
    rows = (iota((8, 128), 0) + LATER) & 7
    rhs, cond, corner = [lines[pl.ds(f, 8, stride=7), :] for f in range(3)]
    from_below = jnp.where(rows > 0, pltpu.roll(corner, 1, 0), 0.0)
    from_above = jnp.where(rows < 7, pltpu.roll(corner, 7, 0), 0.0)
    rhs = rhs + jnp.where(lanes % 64 < 32, from_below, from_above)
    for i in range(ROW):
        column[i * 16 : i * 16 + 8, :] = rhs
        column[i * 16 + 8 : i * 16 + 16, :] = cond


def pass_kernel(gathered, lines, passed, edges):
    own, _, column = place()
    upper = gathered[pl.ds(((4 - SIDE) & 7) * 16, 64), :]
    lower = gathered[pl.ds(((0 - SIDE) & 7) * 16, 64), :]
    passed[...] = jnp.where(column < ROW // 2, upper, lower)
    below = lines[pl.ds(((own + 7 - LATER) & 7) * 7 + 3, 4), :]
    above = lines[pl.ds(((own + 9 - LATER) & 7) * 7 + 3, 4), :]
    edges[0:4, :] = jnp.where(own > 0, below, 0.0)
    edges[4:8, :] = jnp.where(own < 7, above, 0.0)


def fix_kernel(edges, partial, residual):
    rows = iota((8, 128), 0)
    for grid in range(2):
        for x in range(4):
            at = slice(grid * 32 + x * 8, grid * 32 + x * 8 + 8)
            value = partial[at, :]
            if x in (0, 3):
                row = (x // 3) * 2 + grid
                value = value + jnp.where(
                    rows == 0,
                    edges[row : row + 1, :],
                    jnp.where(rows == 7, edges[4 + row : 5 + row, :], 0.0),
                )
            residual[at, :] = value


def coarse_kernel(gathered, extra, smoothed, pressure):
    own, _, column = place()
    lanes = iota((8, 128), 1)
    rows = (iota((8, 128), 0) + LATER) & 7
    low_z = lanes % 32 > 0
    high_z = lanes % 32 < 31
    first_y = lanes % 64 < 32

    def shift_z(value):
        return jnp.where(low_z, pltpu.roll(value, 1, 1), 0.0) + jnp.where(
            high_z, pltpu.roll(value, 127, 1), 0.0
        )

    def shift_y(value):
        ahead = pltpu.roll(value, 96, 1)
        behind = pltpu.roll(value, 32, 1)
        within = jnp.where(first_y, ahead, behind)
        from_below = jnp.where(rows > 0, pltpu.roll(ahead, 1, 0), 0.0)
        from_above = jnp.where(rows < 7, pltpu.roll(behind, 7, 0), 0.0)
        return within + jnp.where(first_y, from_below, from_above)

    rhs, cond = [], []
    for slot in range(7):
        at = column + slot - 3
        inside = jnp.logical_and(at >= 0, at < ROW)
        here = pl.multiple_of(((jnp.clip(at, 0, ROW - 1) - SIDE) & 7) * 16, 16)
        there = pl.multiple_of((at & 3) * 16, 16)
        for f, out in ((0, rhs), (8, cond)):
            out.append(
                jnp.where(inside, gathered[pl.ds(here + f, 8), :], extra[pl.ds(there + f, 8), :])
            )
    scale = [
        jnp.where(c > 0.0, damping / (stencil_weight_sum * coarse_scale * jnp.where(c > 0.0, c, 1.0)), 0.0)
        for c in cond
    ]
    value = [r * s for r, s in zip(rhs, scale)]
    own_sum = [
        half_weight_sum * c + s for c, s in zip(cond[1:-1], neighbour_sums(cond, shift_y, shift_z))
    ]
    for sweep in range(3):
        around = neighbour_sums(value, shift_y, shift_z)
        around_both = neighbour_sums(
            [v * c for v, c in zip(value, cond)], shift_y, shift_z
        )
        value, cond, rhs, scale = value[1:-1], cond[1:-1], rhs[1:-1], scale[1:-1]
        value = [
            v + s * (r - coarse_scale * (v * o - c * a - b))
            for v, s, r, o, c, a, b in zip(value, scale, rhs, own_sum, cond, around, around_both)
        ]
        own_sum = own_sum[1:-1]
    mine = jnp.sum(jnp.where(rows == own, value[0], 0.0), axis=0, keepdims=True)
    spread = jnp.where(iota((16, 128), 0) // 4 == iota((16, 128), 1) // 32, mine, 0.0)
    expand = (iota((128, 128), 0) % 32 == iota((128, 128), 1) // 4).astype(F32)
    fine = jnp.dot(spread, expand, preferred_element_type=F32, precision=lax.Precision.HIGHEST)
    for grid in range(2):
        for x in range(4):
            at = slice(grid * 32 + x * 8, grid * 32 + x * 8 + 8)
            pressure[at, :] = smoothed[at, :] + fine[grid * 8 : grid * 8 + 8]


def call(kernel, name, outs, operands, spaces, scratch=()):
    return pl.pallas_call(
        kernel,
        out_shape=[
            jax.ShapeDtypeStruct(*(out if isinstance(out[0], tuple) else (out, F32))) for out in outs
        ],
        in_specs=[pl.BlockSpec(memory_space=space) for space in spaces],
        out_specs=[pl.BlockSpec(memory_space=pltpu.VMEM)] * len(outs),
        scratch_shapes=scratch,
        compiler_params=pltpu.CompilerParams(vmem_limit_bytes=MEMORY),
        cost_estimate=pl.CostEstimate(flops=1000000, bytes_accessed=200000, transcendentals=0),
        name=name,
    )(*operands)


def local(pressure_rhs, conductivity, block_counts, donor_base, donor_frac, receptor_cells):
    shape = pressure_rhs.shape
    size = lax.axis_size("gx")
    rhs = pressure_rhs.reshape(64, 128)
    cond = conductivity.reshape(64, 128)
    counts = block_counts[0]
    cells = receptor_cells[0, 0]
    base = donor_base[0, 0]
    frac = donor_frac[:, 0, 0]
    vector, far_memory = pltpu.VMEM, pltpu.HBM
    whole = (64, 128)
    smoothed, count, near, far, sent, marked = call(
        front_kernel, "front",
        [whole, whole, (32, 128), (32, 128), (8, 24, 128), ((8, 256), jnp.int32)],
        tuple(
            pltpu.with_memory_space_constraint(value, far_memory)
            for value in (counts, cells, cond, rhs, base, frac)
        ),
        [far_memory] * 6,
        [
            pltpu.SMEM((8, 8), jnp.int32),
            pltpu.VMEM((8, 256), jnp.int32),
            pltpu.VMEM(whole, F32),
            pltpu.VMEM(whole, F32),
            pltpu.VMEM((8, 256), jnp.int32),
            pltpu.VMEM((3, 8, 256), F32),
            pltpu.VMEM((8, 256), F32),
            pltpu.SemaphoreType.DMA((6,)),
        ],
    )
    turned = [[(i + TURN) % 8 for i in range(8)]]
    arrived = lax.all_to_all(
        sent, "gy", split_axis=0, concat_axis=0, tiled=True,
        axis_index_groups=turned,
    )
    beyond = [(i, i + 1) for i in range(1, size - 1, 2)]
    far_in = lax.ppermute(far, "gx", beyond + [(j, i) for i, j in beyond])
    near_in = lax.ppermute(near, "gx", [(i, i ^ 1) for i in range(size)])
    partial, coarse = call(
        residual_kernel, "residual", [whole, (56, 128)],
        (marked, arrived, smoothed, count, rhs, cond, far_in, near_in),
        [vector] * 8,
    )
    lines = lax.all_to_all(
        coarse.reshape(56, 1, 128), "gy", split_axis=0, concat_axis=0, tiled=True,
        axis_index_groups=[[(i + LATER) % 8 for i in range(8)]],
    ).reshape(56, 128)
    (column,) = call(merge_kernel, "merge", [(128, 128)], (lines,), [vector])
    gathered = lax.all_to_all(
        column, "gx", split_axis=0, concat_axis=0, tiled=True,
        axis_index_groups=[
            [start + (i + SIDE) % ROW for i in range(ROW)] for start in range(0, size, ROW)
        ],
    )
    passed, edges = call(
        pass_kernel, "pass", [(64, 128), (8, 128)], (gathered, lines), [vector] * 2
    )
    step = [(i, i + ROW) if i % ROW < ROW // 2 else (i, i - ROW) for i in range(size)]
    extra = lax.ppermute(passed, "gx", [(i, j) for i, j in step if 0 <= j < size])
    (residual,) = call(
        fix_kernel, "fix", [whole], (edges, partial), [vector] * 2
    )
    (pressure,) = call(
        coarse_kernel, "coarse", [whole],
        (gathered, extra, smoothed), [vector] * 3,
    )
    return pressure.reshape(shape), residual.reshape(shape)


def solution(mesh):
    return jax.shard_map(
        local,
        mesh=mesh,
        in_specs=(
            P(None, "gx", "gy", None),
            P(None, "gx", "gy", None),
            P("gx", None, None),
            P("gx", "gy", None, None),
            P(None, "gx", "gy", None, None),
            P("gx", "gy", None, None),
        ),
        out_specs=(P(None, "gx", "gy", None), P(None, "gx", "gy", None)),
        check_vma=False,
    )
```

```python
import functools

import jax
import jax.numpy as jnp
from jax import lax
from jax.experimental import pallas as pl
from jax.experimental.pallas import tpu as pltpu
from jax.sharding import PartitionSpec as P

BLOCK = 128
ROW = 8
TURN = 3
LATER = 4


def side_of(along):
    return 4 * (along >= ROW)


F32 = jnp.float32
BF16 = jnp.bfloat16
damping = 0.8
penalty_weight = 2.0
coarse_scale = 0.0625
stencil_weight_sum = 44.0 / 3.0
half_weight_sum = 22.0 / 3.0
MEMORY = 32 * 1024 * 1024


def iota(shape, axis):
    return lax.broadcasted_iota(jnp.int32, shape, axis)


def place():
    along = lax.axis_index("gx")
    return along, lax.axis_index("gy"), lax.rem(along, 2) == 0


def parts(value, count):
    cuts = []
    for index in range(count):
        cut = value.astype(BF16)
        cuts.append(cut)
        if index + 1 < count:
            value = value - cut.astype(F32)
    return cuts


def one_hots(cells):
    rows = cells.shape[1]
    low = iota((128, rows), 0) == (cells & 127)
    return iota((64, rows), 0) == (cells >> 7), low.astype(F32).astype(BF16)


def contract_rows(left, right):
    return lax.dot_general(left, right, (((1,), (1,)), ((), ())), preferred_element_type=F32)


def front_kernel(
    counts_in, cells_in, cond_in, rhs_in, base_in, frac_in, smoothed, count, near, far, sent,
    marked, counts, cells, cond, rhs, base, frac, donors, sems,
):
    _, own, first = place()
    pairs = (
        (counts_in, counts), (cells_in, cells), (cond_in, cond), (rhs_in, rhs), (base_in, base),
        (frac_in, frac),
    )
    copies = [
        pltpu.make_async_copy(source, target, sems.at[i]) for i, (source, target) in enumerate(pairs)
    ]
    for copy in copies:
        copy.start()
    copies[0].wait()
    copies[1].wait()
    lane = iota((1, 256), 1)
    total = jnp.zeros((64, 128), F32)
    for b in range(8):
        row = jnp.where(lane < counts[b, own] * BLOCK, cells[b : b + 1, :], -BLOCK)
        marked[b : b + 1, :] = row
        high, low = one_hots(row)
        total = total + contract_rows(high.astype(F32).astype(BF16), low)
    count[...] = total
    copies[2].wait()
    copies[3].wait()
    field = damping * rhs[...] / (stencil_weight_sum * cond[...] + penalty_weight * total)
    smoothed[...] = field
    for f, ref in ((0, smoothed), (16, cond)):
        for grid in range(2):
            low_x = ref[grid * 32 : grid * 32 + 8, :]
            high_x = ref[grid * 32 + 24 : grid * 32 + 32, :]
            at = slice(f + grid * 8, f + grid * 8 + 8)
            near[at, :] = jnp.where(first, high_x, low_x)
            far[at, :] = jnp.where(first, low_x, high_x)

    faces = [
        [ref[pl.ds(y, 8, stride=8), :] for ref in (smoothed, cond)] for y in (0, 7)
    ]
    for d in range(8):
        for f in range(2):
            sent[(d - TURN) % 8, f * 8 : f * 8 + 8, :] = jnp.where(d > own, faces[1][f], faces[0][f])

    copies[4].wait()
    copies[5].wait()
    high = field.astype(BF16).astype(F32)
    stacked = jnp.concatenate([high, field - high, high], axis=0)
    columns = stacked.T.astype(BF16)
    q = base[...]
    grid = (q >= 2667).astype(jnp.int32)
    q = q - grid * 2667
    x = (q >= 889).astype(jnp.int32) + (q >= 1778).astype(jnp.int32)
    q = q - x * 889
    y = jnp.zeros_like(q)
    for step in range(1, 7):
        y = y + (q >= step * 127).astype(jnp.int32)
    z = q - y * 127
    plane = grid * 4 + x
    eight = iota((8, 256), 0)
    wide = iota((128, 256), 0)
    for d in range(8):
        row = slice(d, d + 1)
        frac_x, frac_y, frac_z = frac[0, row, :], frac[1, row, :], frac[2, row, :]
        at_x, at_y, at_z = plane[row], y[row], z[row]
        weight_x = jnp.where(eight == at_x, 1.0 - frac_x, jnp.where(eight == at_x + 1, frac_x, 0.0))
        weight_y = jnp.where(eight == at_y, 1.0 - frac_y, jnp.where(eight == at_y + 1, frac_y, 0.0))
        weight_z = jnp.where(wide == at_z, 1.0 - frac_z, jnp.where(wide == at_z + 1, frac_z, 0.0))
        weight = jnp.concatenate([weight_x[p : p + 1] * weight_y for p in range(8)], axis=0)
        upper, lower = parts(weight, 2)
        mixed = jnp.dot(
            columns, jnp.concatenate([upper, upper, lower], axis=0), preferred_element_type=F32
        )
        donors[row, :] = jnp.sum(mixed * weight_z, axis=0, keepdims=True)
    for d in range(8):
        sent[(d - TURN) % 8, 16:17, :] = donors[d : d + 1, 0:128]
        sent[(d - TURN) % 8, 17:18, :] = donors[d : d + 1, 128:256]


def neighbour_sums(fields, shift_y, shift_z):
    inner, outer = [], []
    for field in fields:
        beside_z = shift_z(field)
        beside_y = shift_y(field)
        both = shift_z(beside_y)
        inner.append(0.5 * (beside_z + beside_y) + 0.25 * both)
        outer.append(0.5 * field + 0.25 * (beside_z + beside_y) + (1.0 / 6.0) * both)
    return [inner[i] + outer[i - 1] + outer[i + 1] for i in range(1, len(fields) - 1)]


def residual_kernel(
    cells, arrived, smoothed, count, rhs, cond, far, near, partial, coarse
):
    _, own, first = place()
    total = jnp.zeros((192, 128), F32)
    for b in range(8):
        high, low = one_hots(cells[b : b + 1, :])
        values = jnp.concatenate([arrived[(b - TURN) % 8, 16:17, :], arrived[(b - TURN) % 8, 17:18, :]], axis=1)
        left = jnp.concatenate(
            [jnp.where(high, cut.astype(F32), 0.0).astype(BF16) for cut in parts(values, 3)], axis=0
        )
        total = total + contract_rows(left, low)
    total = total[0:64] + total[64:128] + total[128:192]

    below = jnp.where(own > 0, arrived[(own + 7 - TURN) & 7, 0:16, :], 0.0)
    above = jnp.where(own < 7, arrived[(own + 9 - TURN) & 7, 0:16, :], 0.0)
    lanes = iota((8, 128), 1)
    rows = iota((8, 128), 0)
    keep_up = lanes < 127
    keep_down = lanes > 0

    def shift_z(value):
        return jnp.where(keep_down, pltpu.roll(value, 1, 1), 0.0) + jnp.where(
            keep_up, pltpu.roll(value, 127, 1), 0.0
        )

    def shift_y(value, lower, upper):
        down = jnp.where(rows > 0, pltpu.roll(value, 1, 0), lower)
        up = jnp.where(rows < 7, pltpu.roll(value, 7, 0), upper)
        return down + up

    pooled = []
    for grid in range(2):
        fields = []
        for f, ref in ((0, smoothed), (1, cond)):
            at = slice((2 * f + grid) * 8, (2 * f + grid) * 8 + 8)
            near_plane, far_plane = near[at, :], far[at, :]
            left = jnp.where(first, far_plane, near_plane)
            right = jnp.where(first, near_plane, far_plane)
            start = grid * 32
            planes = [left] + [ref[start + x * 8 : start + x * 8 + 8, :] for x in range(4)] + [right]
            at = 8 * f + grid * 4
            lower = [0.0] + [below[at + x : at + x + 1, :] for x in range(4)] + [0.0]
            upper = [0.0] + [above[at + x : at + x + 1, :] for x in range(4)] + [0.0]
            fields.append((planes, lower, upper))
        fields.append(tuple([v * c for v, c in zip(*pair)] for pair in zip(*fields)))
        sums = []
        for planes, lower, upper in fields:
            inner, outer = [], []
            for plane, low_row, high_row in zip(planes, lower, upper):
                beside_z = shift_z(plane)
                beside_y = shift_y(plane, low_row, high_row)
                both = shift_z(beside_y)
                edge = beside_z + beside_y
                inner.append(0.5 * edge + 0.25 * both)
                outer.append(0.5 * plane + 0.25 * edge + (1.0 / 6.0) * both)
            sums.append([inner[i] + outer[i - 1] + outer[i + 1] for i in range(1, 5)])
        summed = jnp.zeros((8, 128), F32)
        for x in range(4):
            at = slice(grid * 32 + x * 8, grid * 32 + x * 8 + 8)
            v, c = smoothed[at, :], cond[at, :]
            applied = v * (half_weight_sum * c + sums[1][x]) - c * sums[0][x] - sums[2][x]
            value = rhs[at, :] - applied - penalty_weight * (count[at, :] * v - total[at])
            partial[at, :] = value
            summed = summed + value
        pooled.append(summed)
    for grid in range(2):
        start = grid * 32
        pooled.append(sum(cond[start + x * 8 : start + x * 8 + 8, :] for x in range(4)))

    here = []
    there = []
    for f in range(2):
        here.append(
            jnp.concatenate(
                [
                    face[8 * f + 4 * grid + x : 8 * f + 4 * grid + x + 1, :]
                    for face in (below, above)
                    for x in (0, 3)
                    for grid in range(2)
                ],
                axis=0,
            )
        )
        corner = []
        for y in (0, 7):
            near_rows = near[pl.ds(16 * f + y, 2, stride=8), :]
            far_rows = far[pl.ds(16 * f + y, 2, stride=8), :]
            corner.append(jnp.where(first, far_rows, near_rows))
            corner.append(jnp.where(first, near_rows, far_rows))
        there.append(jnp.concatenate(corner, axis=0))

    def corner_sum(value):
        return 0.25 * value + (1.0 / 6.0) * shift_z(value)

    fix = (
        here[1] * corner_sum(there[0])
        + corner_sum(there[0] * there[1])
        - here[0] * corner_sum(there[1])
    )
    pooled.append(fix)
    pool = (iota((128, 128), 0) // 4 == iota((128, 128), 1) % 32).astype(F32)
    means = jnp.dot(
        jnp.concatenate(pooled, axis=0),
        pool,
        preferred_element_type=F32,
        precision=lax.Precision.HIGHEST,
    ) * (1.0 / 64.0)
    own_part = iota((16, 128), 0) // 4 == iota((16, 128), 1) // 32
    lines = [
        jnp.sum(jnp.where(own_part, means[f * 16 : f * 16 + 16], 0.0), axis=0, keepdims=True)
        for f in range(2)
    ]
    fix_part = (rows % 2) * 2 + 1 - rows // 4 == lanes // 32
    lines.append(jnp.sum(jnp.where(fix_part, means[32:40], 0.0), axis=0, keepdims=True))
    tiles = []
    for j in range(8):
        above = (j + LATER) % 8 > own
        tiles += lines + [jnp.where(above, fix[4:8], fix[0:4])]
    coarse[...] = jnp.concatenate(tiles, axis=0)


def merge_kernel(lines, column):
    lanes = iota((8, 128), 1)
    rows = (iota((8, 128), 0) + LATER) & 7
    rhs, cond, corner = [lines[pl.ds(f, 8, stride=7), :] for f in range(3)]
    from_below = jnp.where(rows > 0, pltpu.roll(corner, 1, 0), 0.0)
    from_above = jnp.where(rows < 7, pltpu.roll(corner, 7, 0), 0.0)
    rhs = rhs + jnp.where(lanes % 64 < 32, from_below, from_above)
    for i in range(ROW):
        column[i * 16 : i * 16 + 8, :] = rhs
        column[i * 16 + 8 : i * 16 + 16, :] = cond


def pass_kernel(gathered, lines, passed, edges):
    along, own, _ = place()
    low_half = lax.rem(along, ROW) < ROW // 2
    start = (jnp.where(low_half, ROW // 2, 0) - side_of(along)) & 7
    passed[...] = gathered[pl.ds(pl.multiple_of(start * 16, 64), 64), :]
    below = lines[pl.ds(((own + 7 - LATER) & 7) * 7 + 3, 4), :]
    above = lines[pl.ds(((own + 9 - LATER) & 7) * 7 + 3, 4), :]
    edges[0:4, :] = jnp.where(own > 0, below, 0.0)
    edges[4:8, :] = jnp.where(own < 7, above, 0.0)


def fix_kernel(edges, partial, residual):
    rows = iota((8, 128), 0)
    for grid in range(2):
        for x in range(4):
            at = slice(grid * 32 + x * 8, grid * 32 + x * 8 + 8)
            value = partial[at, :]
            if x in (0, 3):
                row = (x // 3) * 2 + grid
                value = value + jnp.where(
                    rows == 0,
                    edges[row : row + 1, :],
                    jnp.where(rows == 7, edges[4 + row : 5 + row, :], 0.0),
                )
            residual[at, :] = value


def coarse_kernel(gathered, extra, smoothed, pressure):
    along, own, _ = place()
    column, side = lax.rem(along, ROW), side_of(along)
    lanes = iota((8, 128), 1)
    rows = (iota((8, 128), 0) + LATER) & 7
    low_z = lanes % 32 > 0
    high_z = lanes % 32 < 31
    first_y = lanes % 64 < 32

    def shift_z(value):
        return jnp.where(low_z, pltpu.roll(value, 1, 1), 0.0) + jnp.where(
            high_z, pltpu.roll(value, 127, 1), 0.0
        )

    def shift_y(value):
        ahead = pltpu.roll(value, 96, 1)
        behind = pltpu.roll(value, 32, 1)
        within = jnp.where(first_y, ahead, behind)
        from_below = jnp.where(rows > 0, pltpu.roll(ahead, 1, 0), 0.0)
        from_above = jnp.where(rows < 7, pltpu.roll(behind, 7, 0), 0.0)
        return within + jnp.where(first_y, from_below, from_above)

    rhs, cond = [], []
    for slot in range(7):
        at = column + slot - 3
        inside = jnp.logical_and(at >= 0, at < ROW)
        here = pl.multiple_of(((jnp.clip(at, 0, ROW - 1) - side) & 7) * 16, 16)
        there = pl.multiple_of((at & 3) * 16, 16)
        for f, out in ((0, rhs), (8, cond)):
            out.append(
                jnp.where(inside, gathered[pl.ds(here + f, 8), :], extra[pl.ds(there + f, 8), :])
            )
    scale = [
        jnp.where(c > 0.0, damping / (stencil_weight_sum * coarse_scale * jnp.where(c > 0.0, c, 1.0)), 0.0)
        for c in cond
    ]
    value = [r * s for r, s in zip(rhs, scale)]
    own_sum = [
        half_weight_sum * c + s for c, s in zip(cond[1:-1], neighbour_sums(cond, shift_y, shift_z))
    ]
    for sweep in range(3):
        around = neighbour_sums(value, shift_y, shift_z)
        around_both = neighbour_sums(
            [v * c for v, c in zip(value, cond)], shift_y, shift_z
        )
        value, cond, rhs, scale = value[1:-1], cond[1:-1], rhs[1:-1], scale[1:-1]
        value = [
            v + s * (r - coarse_scale * (v * o - c * a - b))
            for v, s, r, o, c, a, b in zip(value, scale, rhs, own_sum, cond, around, around_both)
        ]
        own_sum = own_sum[1:-1]
    mine = jnp.sum(jnp.where(rows == own, value[0], 0.0), axis=0, keepdims=True)
    spread = jnp.where(iota((16, 128), 0) // 4 == iota((16, 128), 1) // 32, mine, 0.0)
    expand = (iota((128, 128), 0) % 32 == iota((128, 128), 1) // 4).astype(F32)
    fine = jnp.dot(spread, expand, preferred_element_type=F32, precision=lax.Precision.HIGHEST)
    for grid in range(2):
        for x in range(4):
            at = slice(grid * 32 + x * 8, grid * 32 + x * 8 + 8)
            pressure[at, :] = smoothed[at, :] + fine[grid * 8 : grid * 8 + 8]


def call(kernel, name, outs, operands, spaces, scratch=()):
    return pl.pallas_call(
        kernel,
        out_shape=[
            jax.ShapeDtypeStruct(*(out if isinstance(out[0], tuple) else (out, F32))) for out in outs
        ],
        in_specs=[pl.BlockSpec(memory_space=space) for space in spaces],
        out_specs=[pl.BlockSpec(memory_space=pltpu.VMEM)] * len(outs),
        scratch_shapes=scratch,
        compiler_params=pltpu.CompilerParams(vmem_limit_bytes=MEMORY),
        cost_estimate=pl.CostEstimate(flops=1000000, bytes_accessed=200000, transcendentals=0),
        name=name,
    )(*operands)


def local(pressure_rhs, conductivity, block_counts, donor_base, donor_frac, receptor_cells):
    shape = pressure_rhs.shape
    size = lax.axis_size("gx")
    rhs = pressure_rhs.reshape(64, 128)
    cond = conductivity.reshape(64, 128)
    counts = block_counts[0]
    cells = receptor_cells[0, 0]
    base = donor_base[0, 0]
    frac = donor_frac[:, 0, 0]
    vector, far_memory = pltpu.VMEM, pltpu.HBM
    whole = (64, 128)
    smoothed, count, near, far, sent, marked = call(
        front_kernel, "front",
        [whole, whole, (32, 128), (32, 128), (8, 24, 128), ((8, 256), jnp.int32)],
        tuple(
            pltpu.with_memory_space_constraint(value, far_memory)
            for value in (counts, cells, cond, rhs, base, frac)
        ),
        [far_memory] * 6,
        [
            pltpu.SMEM((8, 8), jnp.int32),
            pltpu.VMEM((8, 256), jnp.int32),
            pltpu.VMEM(whole, F32),
            pltpu.VMEM(whole, F32),
            pltpu.VMEM((8, 256), jnp.int32),
            pltpu.VMEM((3, 8, 256), F32),
            pltpu.VMEM((8, 256), F32),
            pltpu.SemaphoreType.DMA((6,)),
        ],
    )
    turned = [[(i + TURN) % 8 for i in range(8)]]
    arrived = lax.all_to_all(
        sent, "gy", split_axis=0, concat_axis=0, tiled=True, axis_index_groups=turned
    )
    beyond = [(i, i + 1) for i in range(1, size - 1, 2)]
    far_in = lax.ppermute(far, "gx", beyond + [(j, i) for i, j in beyond])
    near_in = lax.ppermute(near, "gx", [(i, i ^ 1) for i in range(size)])
    partial, coarse = call(
        residual_kernel, "residual", [whole, (56, 128)],
        (marked, arrived, smoothed, count, rhs, cond, far_in, near_in),
        [vector] * 8,
    )
    lines = lax.all_to_all(
        coarse.reshape(56, 1, 128), "gy", split_axis=0, concat_axis=0, tiled=True,
        axis_index_groups=[[(i + LATER) % 8 for i in range(8)]],
    ).reshape(56, 128)
    (column,) = call(merge_kernel, "merge", [(128, 128)], (lines,), [vector])
    gathered = lax.all_to_all(
        column, "gx", split_axis=0, concat_axis=0, tiled=True,
        axis_index_groups=[
            [start + (i + int(side_of(start))) % ROW for i in range(ROW)]
            for start in range(0, size, ROW)
        ],
    )
    passed, edges = call(
        pass_kernel, "pass", [(64, 128), (8, 128)], (gathered, lines), [vector] * 2
    )
    step = [(i, i + ROW) if i % ROW < ROW // 2 else (i, i - ROW) for i in range(size)]
    extra = lax.ppermute(passed, "gx", [(i, j) for i, j in step if 0 <= j < size])
    (residual,) = call(
        fix_kernel, "fix", [whole], (edges, partial), [vector] * 2
    )
    (pressure,) = call(
        coarse_kernel, "coarse", [whole],
        (gathered, extra, smoothed), [vector] * 3,
    )
    return pressure.reshape(shape), residual.reshape(shape)


def solution(mesh):
    return jax.shard_map(
        local,
        mesh=mesh,
        in_specs=(
            P(None, "gx", "gy", None),
            P(None, "gx", "gy", None),
            P("gx", None, None),
            P("gx", "gy", None, None),
            P(None, "gx", "gy", None, None),
            P("gx", "gy", None, None),
        ),
        out_specs=(P(None, "gx", "gy", None), P(None, "gx", "gy", None)),
        check_vma=False,
    )
```

```python
import functools

import jax
import jax.numpy as jnp
from jax import lax
from jax.experimental import pallas as pl
from jax.experimental.pallas import tpu as pltpu
from jax.sharding import PartitionSpec as P

BLOCK = 128
ROW = 8
TURN = 5
CHUNK = 26
LATER = 4


def side_of(along):
    return 4 * (along >= ROW)


F32 = jnp.float32
BF16 = jnp.bfloat16
damping = 0.8
penalty_weight = 2.0
coarse_scale = 0.0625
stencil_weight_sum = 44.0 / 3.0
half_weight_sum = 22.0 / 3.0
MEMORY = 32 * 1024 * 1024


def iota(shape, axis):
    return lax.broadcasted_iota(jnp.int32, shape, axis)


def place():
    along = lax.axis_index("gx")
    return along, lax.axis_index("gy"), lax.rem(along, 2) == 0


def parts(value, count):
    cuts = []
    for index in range(count):
        cut = value.astype(BF16)
        cuts.append(cut)
        if index + 1 < count:
            value = value - cut.astype(F32)
    return cuts


def one_hots(cells):
    rows = cells.shape[1]
    low = iota((128, rows), 0) == (cells & 127)
    return iota((64, rows), 0) == (cells >> 7), low.astype(F32).astype(BF16)


def exact_product(value, table):
    rows = value.shape[0]
    cuts = jnp.dot(
        jnp.concatenate(parts(value, 3), axis=0), table.astype(F32).astype(BF16),
        preferred_element_type=F32,
    )
    return cuts[0:rows] + cuts[rows : 2 * rows] + cuts[2 * rows : 3 * rows]


def contract_rows(left, right):
    return lax.dot_general(left, right, (((1,), (1,)), ((), ())), preferred_element_type=F32)


def front_kernel(
    counts_in, cells_in, cond_in, rhs_in, smoothed, count, near, far, marked,
    counts, cells, cond, rhs, sems,
):
    _, own, first = place()
    pairs = ((counts_in, counts), (cells_in, cells), (cond_in, cond), (rhs_in, rhs))
    copies = [
        pltpu.make_async_copy(source, target, sems.at[i]) for i, (source, target) in enumerate(pairs)
    ]
    for copy in copies:
        copy.start()
    copies[0].wait()
    copies[1].wait()
    lane = iota((1, 256), 1)
    total = jnp.zeros((64, 128), F32)
    for b in range(8):
        row = jnp.where(lane < counts[b, own] * BLOCK, cells[b : b + 1, :], -BLOCK)
        marked[b : b + 1, :] = row
        high, low = one_hots(row)
        total = total + contract_rows(high.astype(F32).astype(BF16), low)
    count[...] = total
    copies[2].wait()
    copies[3].wait()
    field = damping * rhs[...] / (stencil_weight_sum * cond[...] + penalty_weight * total)
    smoothed[...] = field
    for f, ref in ((0, smoothed), (16, cond)):
        for grid in range(2):
            low_x = ref[grid * 32 : grid * 32 + 8, :]
            high_x = ref[grid * 32 + 24 : grid * 32 + 32, :]
            at = slice(f + grid * 8, f + grid * 8 + 8)
            near[at, :] = jnp.where(first, high_x, low_x)
            far[at, :] = jnp.where(first, low_x, high_x)


def donor_kernel(base, frac, smoothed, donors):
    field = smoothed[...]
    high = field.astype(BF16).astype(F32)
    stacked = jnp.concatenate([high, field - high, high], axis=0)
    columns = stacked.T.astype(BF16)
    q = base[...]
    grid = (q >= 2667).astype(jnp.int32)
    q = q - grid * 2667
    x = (q >= 889).astype(jnp.int32) + (q >= 1778).astype(jnp.int32)
    q = q - x * 889
    y = jnp.zeros_like(q)
    for step in range(1, 7):
        y = y + (q >= step * 127).astype(jnp.int32)
    z = q - y * 127
    plane = grid * 4 + x
    eight = iota((8, 256), 0)
    wide = iota((128, 256), 0)
    for d in range(8):
        row = slice(d, d + 1)
        frac_x, frac_y, frac_z = frac[0, row, :], frac[1, row, :], frac[2, row, :]
        at_x, at_y, at_z = plane[row], y[row], z[row]
        weight_x = jnp.where(eight == at_x, 1.0 - frac_x, jnp.where(eight == at_x + 1, frac_x, 0.0))
        weight_y = jnp.where(eight == at_y, 1.0 - frac_y, jnp.where(eight == at_y + 1, frac_y, 0.0))
        weight_z = jnp.where(wide == at_z, 1.0 - frac_z, jnp.where(wide == at_z + 1, frac_z, 0.0))
        weight = jnp.concatenate([weight_x[p : p + 1] * weight_y for p in range(8)], axis=0)
        upper, lower = parts(weight, 2)
        mixed = jnp.dot(
            columns, jnp.concatenate([upper, upper, lower], axis=0), preferred_element_type=F32
        )
        donors[row, :] = jnp.sum(mixed * weight_z, axis=0, keepdims=True)


def pack_kernel(donors, smoothed, cond, far, near, sent):
    _, own, first = place()
    faces = []
    for y in (0, 7):
        near_rows = near[pl.ds(y, 4, stride=8), :]
        far_rows = far[pl.ds(y, 4, stride=8), :]
        faces.append(
            (
                smoothed[pl.ds(y, 8, stride=8), :],
                cond[pl.ds(y, 8, stride=8), :],
                jnp.where(first, far_rows, near_rows),
                jnp.where(first, near_rows, far_rows),
            )
        )
    for d in range(8):
        start = (d - TURN) % 8 * CHUNK
        for f, (row, count) in enumerate(((0, 8), (8, 8), (16, 4), (20, 4))):
            sent[start + row : start + row + count, :] = jnp.where(
                d > own, faces[1][f], faces[0][f]
            )
        sent[start + 24 : start + 25, :] = donors[d : d + 1, 0:128]
        sent[start + 25 : start + 26, :] = donors[d : d + 1, 128:256]


def neighbour_sums(fields, shift_y, shift_z):
    inner, outer = [], []
    for field in fields:
        beside_z = shift_z(field)
        beside_y = shift_y(field)
        both = shift_z(beside_y)
        inner.append(0.5 * (beside_z + beside_y) + 0.25 * both)
        outer.append(0.5 * field + 0.25 * (beside_z + beside_y) + (1.0 / 6.0) * both)
    return [inner[i] + outer[i - 1] + outer[i + 1] for i in range(1, len(fields) - 1)]


def residual_kernel(
    cells, arrived, smoothed, count, rhs, cond, far, near, partial, coarse
):
    _, own, first = place()
    total = jnp.zeros((128, 128), F32)
    for b in range(8):
        high, low = one_hots(cells[b : b + 1, :])
        values = jnp.concatenate([
                arrived[(b - TURN) % 8 * CHUNK + row : (b - TURN) % 8 * CHUNK + row + 1, :]
                for row in (24, 25)
            ], axis=1)
        left = jnp.concatenate(
            [jnp.where(high, cut.astype(F32), 0.0).astype(BF16) for cut in parts(values, 2)], axis=0
        )
        total = total + contract_rows(left, low)
    total = total[0:64] + total[64:128]

    below = jnp.where(own > 0, arrived[pl.ds(((own + 7 - TURN) & 7) * CHUNK, 24), :], 0.0)
    above = jnp.where(own < 7, arrived[pl.ds(((own + 9 - TURN) & 7) * CHUNK, 24), :], 0.0)
    lanes = iota((8, 128), 1)
    rows = iota((8, 128), 0)
    keep_up = lanes < 127
    keep_down = lanes > 0

    def shift_z(value):
        return jnp.where(keep_down, pltpu.roll(value, 1, 1), 0.0) + jnp.where(
            keep_up, pltpu.roll(value, 127, 1), 0.0
        )

    def shift_y(value, lower, upper):
        down = jnp.where(rows > 0, pltpu.roll(value, 1, 0), lower)
        up = jnp.where(rows < 7, pltpu.roll(value, 7, 0), upper)
        return down + up

    pooled = []
    for grid in range(2):
        fields = []
        for f, ref in ((0, smoothed), (1, cond)):
            at = slice((2 * f + grid) * 8, (2 * f + grid) * 8 + 8)
            near_plane, far_plane = near[at, :], far[at, :]
            left = jnp.where(first, far_plane, near_plane)
            right = jnp.where(first, near_plane, far_plane)
            start = grid * 32
            planes = [left] + [ref[start + x * 8 : start + x * 8 + 8, :] for x in range(4)] + [right]
            at = [16 + 2 * f + grid] + [8 * f + grid * 4 + x for x in range(4)] + [20 + 2 * f + grid]
            lower = [below[row : row + 1, :] for row in at]
            upper = [above[row : row + 1, :] for row in at]
            fields.append((planes, lower, upper))
        fields.append(tuple([v * c for v, c in zip(*pair)] for pair in zip(*fields)))
        sums = []
        for planes, lower, upper in fields:
            inner, outer = [], []
            for plane, low_row, high_row in zip(planes, lower, upper):
                beside_z = shift_z(plane)
                beside_y = shift_y(plane, low_row, high_row)
                both = shift_z(beside_y)
                edge = beside_z + beside_y
                inner.append(0.5 * edge + 0.25 * both)
                outer.append(0.5 * plane + 0.25 * edge + (1.0 / 6.0) * both)
            sums.append([inner[i] + outer[i - 1] + outer[i + 1] for i in range(1, 5)])
        summed = jnp.zeros((8, 128), F32)
        for x in range(4):
            at = slice(grid * 32 + x * 8, grid * 32 + x * 8 + 8)
            v, c = smoothed[at, :], cond[at, :]
            applied = v * (half_weight_sum * c + sums[1][x]) - c * sums[0][x] - sums[2][x]
            value = rhs[at, :] - applied - penalty_weight * (count[at, :] * v - total[at])
            partial[at, :] = value
            summed = summed + value
        pooled.append(summed)
    for grid in range(2):
        start = grid * 32
        pooled.append(sum(cond[start + x * 8 : start + x * 8 + 8, :] for x in range(4)))

    pool = iota((128, 128), 0) // 4 == iota((128, 128), 1) % 32
    means = exact_product(jnp.concatenate(pooled, axis=0), pool) * (1.0 / 64.0)
    own_part = iota((16, 128), 0) // 4 == iota((16, 128), 1) // 32
    lines = [
        jnp.sum(jnp.where(own_part, means[f * 16 : f * 16 + 16], 0.0), axis=0, keepdims=True)
        for f in range(2)
    ]
    coarse[...] = jnp.broadcast_to(jnp.concatenate(lines, axis=0)[None], (64, 2, 128))


def pass_kernel(gathered, passed, token):
    along, _, _ = place()
    low_half = lax.rem(along, ROW) < ROW // 2
    start = (jnp.where(low_half, ROW // 2, 0) - side_of(along)) & 7
    passed[...] = gathered[pl.ds(pl.multiple_of(start * 16, 64), 64), :]
    token[...] = gathered[0:8, :]


def store_kernel(token, partial, residual):
    residual[...] = partial[...]


def coarse_kernel(gathered, extra, smoothed, pressure):
    along, own, _ = place()
    column, side = lax.rem(along, ROW), side_of(along)
    lanes = iota((8, 128), 1)
    rows = (iota((8, 128), 0) + LATER) & 7
    low_z = lanes % 32 > 0
    high_z = lanes % 32 < 31
    first_y = lanes % 64 < 32

    def shift_z(value):
        return jnp.where(low_z, pltpu.roll(value, 1, 1), 0.0) + jnp.where(
            high_z, pltpu.roll(value, 127, 1), 0.0
        )

    def shift_y(value):
        ahead = pltpu.roll(value, 96, 1)
        behind = pltpu.roll(value, 32, 1)
        within = jnp.where(first_y, ahead, behind)
        from_below = jnp.where(rows > 0, pltpu.roll(ahead, 1, 0), 0.0)
        from_above = jnp.where(rows < 7, pltpu.roll(behind, 7, 0), 0.0)
        return within + jnp.where(first_y, from_below, from_above)

    rhs, cond = [], []
    for slot in range(7):
        at = column + slot - 3
        inside = jnp.logical_and(at >= 0, at < ROW)
        here = pl.multiple_of(((jnp.clip(at, 0, ROW - 1) - side) & 7) * 16, 16)
        there = pl.multiple_of((at & 3) * 16, 16)
        for f, out in ((0, rhs), (1, cond)):
            out.append(
                jnp.where(inside, gathered[pl.ds(here + f, 8, stride=2), :],
                    extra[pl.ds(there + f, 8, stride=2), :],)
            )
    scale = [
        jnp.where(c > 0.0, damping / (stencil_weight_sum * coarse_scale * jnp.where(c > 0.0, c, 1.0)), 0.0)
        for c in cond
    ]
    value = [r * s for r, s in zip(rhs, scale)]
    own_sum = [
        half_weight_sum * c + s for c, s in zip(cond[1:-1], neighbour_sums(cond, shift_y, shift_z))
    ]
    for sweep in range(3):
        around = neighbour_sums(value, shift_y, shift_z)
        around_both = neighbour_sums(
            [v * c for v, c in zip(value, cond)], shift_y, shift_z
        )
        value, cond, rhs, scale = value[1:-1], cond[1:-1], rhs[1:-1], scale[1:-1]
        value = [
            v + s * (r - coarse_scale * (v * o - c * a - b))
            for v, s, r, o, c, a, b in zip(value, scale, rhs, own_sum, cond, around, around_both)
        ]
        own_sum = own_sum[1:-1]
    mine = jnp.sum(jnp.where(rows == own, value[0], 0.0), axis=0, keepdims=True)
    spread = jnp.where(iota((16, 128), 0) // 4 == iota((16, 128), 1) // 32, mine, 0.0)
    expand = iota((128, 128), 0) % 32 == iota((128, 128), 1) // 4
    fine = exact_product(spread, expand)
    for grid in range(2):
        for x in range(4):
            at = slice(grid * 32 + x * 8, grid * 32 + x * 8 + 8)
            pressure[at, :] = smoothed[at, :] + fine[grid * 8 : grid * 8 + 8]


def call(kernel, name, outs, operands, spaces, scratch=()):
    return pl.pallas_call(
        kernel,
        out_shape=[
            jax.ShapeDtypeStruct(*(out if isinstance(out[0], tuple) else (out, F32))) for out in outs
        ],
        in_specs=[pl.BlockSpec(memory_space=space) for space in spaces],
        out_specs=[pl.BlockSpec(memory_space=pltpu.VMEM)] * len(outs),
        scratch_shapes=scratch,
        compiler_params=pltpu.CompilerParams(vmem_limit_bytes=MEMORY),
        cost_estimate=pl.CostEstimate(flops=1000000, bytes_accessed=200000, transcendentals=0),
        name=name,
    )(*operands)


def local(pressure_rhs, conductivity, block_counts, donor_base, donor_frac, receptor_cells):
    shape = pressure_rhs.shape
    size = lax.axis_size("gx")
    rhs = pressure_rhs.reshape(64, 128)
    cond = conductivity.reshape(64, 128)
    counts = block_counts[0]
    cells = receptor_cells[0, 0]
    base = donor_base[0, 0]
    frac = donor_frac[:, 0, 0]
    vector, far_memory = pltpu.VMEM, pltpu.HBM
    whole = (64, 128)
    smoothed, count, near, far, marked = call(
        front_kernel, "front",
        [whole, whole, (32, 128), (32, 128), ((8, 256), jnp.int32)],
        tuple(
            pltpu.with_memory_space_constraint(value, far_memory)
            for value in (counts, cells, cond, rhs)
        ),
        [far_memory] * 4,
        [
            pltpu.SMEM((8, 8), jnp.int32),
            pltpu.VMEM((8, 256), jnp.int32),
            pltpu.VMEM(whole, F32),
            pltpu.VMEM(whole, F32),
            pltpu.SemaphoreType.DMA((4,)),
        ],
    )
    beyond = [(i, i + 1) for i in range(1, size - 1, 2)]
    far_in = lax.ppermute(far, "gx", beyond + [(j, i) for i, j in beyond])
    near_in = lax.ppermute(near, "gx", [(i, i ^ 1) for i in range(size)])
    (donors,) = call(donor_kernel, "donor", [(8, 256)], (base, frac, smoothed), [vector] * 3)
    (sent,) = call(
        pack_kernel, "pack", [(8 * CHUNK, 128)], (donors, smoothed, cond, far_in, near_in),
        [vector] * 5,
    )
    arrived = lax.all_to_all(
        sent.reshape(8 * CHUNK, 1, 128), "gy", split_axis=0, concat_axis=0, tiled=True,
        axis_index_groups=[[(i + TURN) % 8 for i in range(8)]],
    ).reshape(8 * CHUNK, 128)
    partial, coarse = call(
        residual_kernel, "residual", [whole, (64, 2, 128)],
        (marked, arrived, smoothed, count, rhs, cond, far_in, near_in), [vector] * 8,
    )
    groups = [
        [
            (start + (i + int(side_of(start))) % ROW) * 8 + (j + LATER) % 8
            for i in range(ROW)
            for j in range(8)
        ]
        for start in range(0, size, ROW)
    ]
    gathered = lax.all_to_all(
        coarse, ("gx", "gy"), split_axis=0, concat_axis=0, tiled=True, axis_index_groups=groups
    ).reshape(128, 128)
    passed, token = call(
        pass_kernel, "pass", [(64, 128), (8, 128)], (gathered,), [vector]
    )
    step = [(i, i + ROW) if i % ROW < ROW // 2 else (i, i - ROW) for i in range(size)]
    extra = lax.ppermute(passed, "gx", [(i, j) for i, j in step if 0 <= j < size])
    (residual,) = call(store_kernel, "store", [whole], (token, partial), [vector] * 2)
    (pressure,) = call(
        coarse_kernel, "coarse", [whole],
        (gathered, extra, smoothed), [vector] * 3,
    )
    return pressure.reshape(shape), residual.reshape(shape)


def solution(mesh):
    return jax.shard_map(
        local,
        mesh=mesh,
        in_specs=(
            P(None, "gx", "gy", None),
            P(None, "gx", "gy", None),
            P("gx", None, None),
            P("gx", "gy", None, None),
            P(None, "gx", "gy", None, None),
            P("gx", "gy", None, None),
        ),
        out_specs=(P(None, "gx", "gy", None), P(None, "gx", "gy", None)),
        check_vma=False,
    )
```

```python
import functools

import jax
import jax.numpy as jnp
from jax import lax
from jax.experimental import pallas as pl
from jax.experimental.pallas import tpu as pltpu
from jax.sharding import PartitionSpec as P

BLOCK = 128
ROW = 8
TURN = 5
CHUNK = 26
LATER = 4


def side_of(along):
    return 4 * (along >= ROW)


F32 = jnp.float32
BF16 = jnp.bfloat16
damping = 0.8
penalty_weight = 2.0
coarse_scale = 0.0625
stencil_weight_sum = 44.0 / 3.0
half_weight_sum = 22.0 / 3.0
MEMORY = 32 * 1024 * 1024


def iota(shape, axis):
    return lax.broadcasted_iota(jnp.int32, shape, axis)


def place():
    along = lax.axis_index("gx")
    return along, lax.axis_index("gy"), lax.rem(along, 2) == 0


def parts(value, count):
    cuts = []
    for index in range(count):
        cut = value.astype(BF16)
        cuts.append(cut)
        if index + 1 < count:
            value = value - cut.astype(F32)
    return cuts


def one_hots(cells):
    rows = cells.shape[1]
    low = iota((128, rows), 0) == (cells & 127)
    return iota((64, rows), 0) == (cells >> 7), low.astype(F32).astype(BF16)


def exact_product(value, table):
    rows = value.shape[0]
    cuts = jnp.dot(
        jnp.concatenate(parts(value, 3), axis=0), table.astype(F32).astype(BF16),
        preferred_element_type=F32,
    )
    return cuts[0:rows] + cuts[rows : 2 * rows] + cuts[2 * rows : 3 * rows]


def contract_rows(left, right):
    return lax.dot_general(left, right, (((1,), (1,)), ((), ())), preferred_element_type=F32)


def front_kernel(
    counts_in, cells_in, cond_in, rhs_in, smoothed, count, near, far, marked,
    counts, cells, cond, rhs, sems,
):
    _, own, first = place()
    pairs = ((counts_in, counts), (cells_in, cells), (cond_in, cond), (rhs_in, rhs))
    copies = [
        pltpu.make_async_copy(source, target, sems.at[i]) for i, (source, target) in enumerate(pairs)
    ]
    for copy in copies:
        copy.start()
    copies[0].wait()
    copies[1].wait()
    lane = iota((1, 256), 1)
    total = jnp.zeros((64, 128), F32)
    for b in range(8):
        row = jnp.where(lane < counts[b, own] * BLOCK, cells[b : b + 1, :], -BLOCK)
        marked[b : b + 1, :] = row
        high, low = one_hots(row)
        total = total + contract_rows(high.astype(F32).astype(BF16), low)
    count[...] = total
    copies[2].wait()
    copies[3].wait()
    field = damping * rhs[...] / (stencil_weight_sum * cond[...] + penalty_weight * total)
    smoothed[...] = field
    for f, ref in ((0, smoothed), (16, cond)):
        for grid in range(2):
            low_x = ref[grid * 32 : grid * 32 + 8, :]
            high_x = ref[grid * 32 + 24 : grid * 32 + 32, :]
            at = slice(f + grid * 8, f + grid * 8 + 8)
            near[at, :] = jnp.where(first, high_x, low_x)
            far[at, :] = jnp.where(first, low_x, high_x)


def donor_kernel(base, frac, smoothed, donors):
    field = smoothed[...]
    high = field.astype(BF16).astype(F32)
    stacked = jnp.concatenate([high, field - high, high], axis=0)
    columns = stacked.T.astype(BF16)
    q = base[...]
    grid = (q >= 2667).astype(jnp.int32)
    q = q - grid * 2667
    x = (q >= 889).astype(jnp.int32) + (q >= 1778).astype(jnp.int32)
    q = q - x * 889
    y = jnp.zeros_like(q)
    for step in range(1, 7):
        y = y + (q >= step * 127).astype(jnp.int32)
    z = q - y * 127
    plane = grid * 4 + x
    eight = iota((8, 256), 0)
    wide = iota((128, 256), 0)
    for d in range(8):
        row = slice(d, d + 1)
        frac_x, frac_y, frac_z = frac[0, row, :], frac[1, row, :], frac[2, row, :]
        at_x, at_y, at_z = plane[row], y[row], z[row]
        weight_x = jnp.where(eight == at_x, 1.0 - frac_x, jnp.where(eight == at_x + 1, frac_x, 0.0))
        weight_y = jnp.where(eight == at_y, 1.0 - frac_y, jnp.where(eight == at_y + 1, frac_y, 0.0))
        weight_z = jnp.where(wide == at_z, 1.0 - frac_z, jnp.where(wide == at_z + 1, frac_z, 0.0))
        weight = jnp.concatenate([weight_x[p : p + 1] * weight_y for p in range(8)], axis=0)
        upper, lower = parts(weight, 2)
        mixed = jnp.dot(
            columns, jnp.concatenate([upper, upper, lower], axis=0), preferred_element_type=F32
        )
        donors[row, :] = jnp.sum(mixed * weight_z, axis=0, keepdims=True)


def pack_kernel(donors, smoothed, cond, far, near, sent):
    _, own, first = place()
    faces = []
    for y in (0, 7):
        near_rows = near[pl.ds(y, 4, stride=8), :]
        far_rows = far[pl.ds(y, 4, stride=8), :]
        faces.append(
            (
                smoothed[pl.ds(y, 8, stride=8), :],
                cond[pl.ds(y, 8, stride=8), :],
                jnp.where(first, far_rows, near_rows),
                jnp.where(first, near_rows, far_rows),
            )
        )
    for d in range(8):
        start = (d - TURN) % 8 * CHUNK
        for f, (row, count) in enumerate(((0, 8), (8, 8), (16, 4), (20, 4))):
            sent[start + row : start + row + count, :] = jnp.where(
                d > own, faces[1][f], faces[0][f]
            )
        sent[start + 24 : start + 25, :] = donors[d : d + 1, 0:128]
        sent[start + 25 : start + 26, :] = donors[d : d + 1, 128:256]


def residual_kernel(
    cells, arrived, smoothed, count, rhs, cond, far, near, partial, coarse
):
    _, own, first = place()
    total = jnp.zeros((128, 128), F32)
    for b in range(8):
        high, low = one_hots(cells[b : b + 1, :])
        values = jnp.concatenate([
                arrived[(b - TURN) % 8 * CHUNK + row : (b - TURN) % 8 * CHUNK + row + 1, :]
                for row in (24, 25)
            ], axis=1)
        left = jnp.concatenate(
            [jnp.where(high, cut.astype(F32), 0.0).astype(BF16) for cut in parts(values, 2)], axis=0
        )
        total = total + contract_rows(left, low)
    total = total[0:64] + total[64:128]

    below = jnp.where(own > 0, arrived[pl.ds(((own + 7 - TURN) & 7) * CHUNK, 24), :], 0.0)
    above = jnp.where(own < 7, arrived[pl.ds(((own + 9 - TURN) & 7) * CHUNK, 24), :], 0.0)
    lanes = iota((8, 128), 1)
    rows = iota((8, 128), 0)
    keep_up = lanes < 127
    keep_down = lanes > 0

    def shift_z(value):
        return jnp.where(keep_down, pltpu.roll(value, 1, 1), 0.0) + jnp.where(
            keep_up, pltpu.roll(value, 127, 1), 0.0
        )

    def shift_y(value, lower, upper):
        down = jnp.where(rows > 0, pltpu.roll(value, 1, 0), lower)
        up = jnp.where(rows < 7, pltpu.roll(value, 7, 0), upper)
        return down + up

    pooled = []
    for grid in range(2):
        fields = []
        for f, ref in ((0, smoothed), (1, cond)):
            at = slice((2 * f + grid) * 8, (2 * f + grid) * 8 + 8)
            near_plane, far_plane = near[at, :], far[at, :]
            left = jnp.where(first, far_plane, near_plane)
            right = jnp.where(first, near_plane, far_plane)
            start = grid * 32
            planes = [left] + [ref[start + x * 8 : start + x * 8 + 8, :] for x in range(4)] + [right]
            at = [16 + 2 * f + grid] + [8 * f + grid * 4 + x for x in range(4)] + [20 + 2 * f + grid]
            lower = [below[row : row + 1, :] for row in at]
            upper = [above[row : row + 1, :] for row in at]
            fields.append((planes, lower, upper))
        fields.append(tuple([v * c for v, c in zip(*pair)] for pair in zip(*fields)))
        sums = []
        for planes, lower, upper in fields:
            inner, outer = [], []
            for plane, low_row, high_row in zip(planes, lower, upper):
                beside_z = shift_z(plane)
                beside_y = shift_y(plane, low_row, high_row)
                both = shift_z(beside_y)
                edge = beside_z + beside_y
                inner.append(0.5 * edge + 0.25 * both)
                outer.append(0.5 * plane + 0.25 * edge + (1.0 / 6.0) * both)
            sums.append([inner[i] + outer[i - 1] + outer[i + 1] for i in range(1, 5)])
        summed = jnp.zeros((8, 128), F32)
        for x in range(4):
            at = slice(grid * 32 + x * 8, grid * 32 + x * 8 + 8)
            v, c = smoothed[at, :], cond[at, :]
            applied = v * (half_weight_sum * c + sums[1][x]) - c * sums[0][x] - sums[2][x]
            value = rhs[at, :] - applied - penalty_weight * (count[at, :] * v - total[at])
            partial[at, :] = value
            summed = summed + value
        pooled.append(summed)
    for grid in range(2):
        start = grid * 32
        pooled.append(sum(cond[start + x * 8 : start + x * 8 + 8, :] for x in range(4)))

    pool = iota((128, 128), 0) // 4 == iota((128, 128), 1) % 32
    means = exact_product(jnp.concatenate(pooled, axis=0), pool) * (1.0 / 64.0)
    own_part = iota((16, 128), 0) // 4 == iota((16, 128), 1) // 32
    lines = [
        jnp.sum(jnp.where(own_part, means[f * 16 : f * 16 + 16], 0.0), axis=0, keepdims=True)
        for f in range(2)
    ]
    coarse[...] = jnp.broadcast_to(jnp.concatenate(lines, axis=0)[None], (64, 2, 128))


def pass_kernel(gathered, passed, token):
    along, _, _ = place()
    low_half = lax.rem(along, ROW) < ROW // 2
    start = (jnp.where(low_half, ROW // 2, 0) ^ side_of(along)) & 4
    start = start * 16 + jnp.where(low_half, 16, 0)
    passed[...] = gathered[pl.ds(pl.multiple_of(start, 16), 48), :]
    token[...] = gathered[0:8, :]


def store_kernel(token, partial, residual):
    residual[...] = partial[...]


def coarse_kernel(gathered, extra, smoothed, pressure):
    along, own, _ = place()
    column, side = lax.rem(along, ROW), side_of(along)
    skip = jnp.where(column < ROW // 2, 1, 0)
    lanes = iota((8, 128), 1)
    rows = (iota((8, 128), 0) + LATER) & 7
    low_z = lanes % 32 > 0
    high_z = lanes % 32 < 31
    first_y = lanes % 64 < 32

    def shift_z(value):
        return jnp.where(low_z, pltpu.roll(value, 1, 1), 0.0) + jnp.where(
            high_z, pltpu.roll(value, 127, 1), 0.0
        )

    def shift_y(value):
        ahead = pltpu.roll(value, 96, 1)
        behind = pltpu.roll(value, 32, 1)
        within = jnp.where(first_y, ahead, behind)
        from_below = jnp.where(rows > 0, pltpu.roll(ahead, 1, 0), 0.0)
        from_above = jnp.where(rows < 7, pltpu.roll(behind, 7, 0), 0.0)
        return within + jnp.where(first_y, from_below, from_above)

    def neighbour_sums(fields):
        sums = []
        for i in range(1, len(fields) - 1):
            field, beside = fields[i], fields[i - 1] + fields[i + 1]
            edge = 0.5 * field + 0.25 * beside
            corner = 0.25 * field + (1.0 / 6.0) * beside
            sums.append(0.5 * beside + shift_y(edge) + shift_z(edge + shift_y(corner)))
        return sums

    rhs, cond = [], []
    for slot in range(7):
        at = column + slot - 3
        inside = jnp.logical_and(at >= 0, at < ROW)
        here = pl.multiple_of((jnp.clip(at, 0, ROW - 1) ^ side) * 16, 16)
        there = pl.multiple_of(jnp.clip((at & 3) - skip, 0, 2) * 16, 16)
        for f, out in ((0, rhs), (1, cond)):
            out.append(
                jnp.where(inside, gathered[pl.ds(here + f, 8, stride=2), :],
                    extra[pl.ds(there + f, 8, stride=2), :],)
            )
    scale = [
        jnp.where(c > 0.0, damping / (stencil_weight_sum * coarse_scale * jnp.where(c > 0.0, c, 1.0)), 0.0)
        for c in cond
    ]
    value = [r * s for r, s in zip(rhs, scale)]
    own_sum = [
        half_weight_sum * c + s for c, s in zip(cond[1:-1], neighbour_sums(cond))
    ]
    for sweep in range(3):
        around = neighbour_sums(value)
        around_both = neighbour_sums([v * c for v, c in zip(value, cond)])
        value, cond, rhs, scale = value[1:-1], cond[1:-1], rhs[1:-1], scale[1:-1]
        value = [
            v + s * (r - coarse_scale * (v * o - c * a - b))
            for v, s, r, o, c, a, b in zip(value, scale, rhs, own_sum, cond, around, around_both)
        ]
        own_sum = own_sum[1:-1]
    mine = jnp.sum(jnp.where(rows == own, value[0], 0.0), axis=0, keepdims=True)
    spread = jnp.where(iota((16, 128), 0) // 4 == iota((16, 128), 1) // 32, mine, 0.0)
    expand = iota((128, 128), 0) % 32 == iota((128, 128), 1) // 4
    fine = exact_product(spread, expand)
    for grid in range(2):
        for x in range(4):
            at = slice(grid * 32 + x * 8, grid * 32 + x * 8 + 8)
            pressure[at, :] = smoothed[at, :] + fine[grid * 8 : grid * 8 + 8]


def call(kernel, name, outs, operands, spaces, scratch=()):
    return pl.pallas_call(
        kernel,
        out_shape=[
            jax.ShapeDtypeStruct(*(out if isinstance(out[0], tuple) else (out, F32))) for out in outs
        ],
        in_specs=[pl.BlockSpec(memory_space=space) for space in spaces],
        out_specs=[pl.BlockSpec(memory_space=pltpu.VMEM)] * len(outs),
        scratch_shapes=scratch,
        compiler_params=pltpu.CompilerParams(vmem_limit_bytes=MEMORY),
        cost_estimate=pl.CostEstimate(flops=1000000, bytes_accessed=200000, transcendentals=0),
        name=name,
    )(*operands)


def local(pressure_rhs, conductivity, block_counts, donor_base, donor_frac, receptor_cells):
    shape = pressure_rhs.shape
    size = lax.axis_size("gx")
    rhs = pressure_rhs.reshape(64, 128)
    cond = conductivity.reshape(64, 128)
    counts = block_counts[0]
    cells = receptor_cells[0, 0]
    base = donor_base[0, 0]
    frac = donor_frac[:, 0, 0]
    vector, far_memory = pltpu.VMEM, pltpu.HBM
    whole = (64, 128)
    smoothed, count, near, far, marked = call(
        front_kernel, "front",
        [whole, whole, (32, 128), (32, 128), ((8, 256), jnp.int32)],
        tuple(
            pltpu.with_memory_space_constraint(value, far_memory)
            for value in (counts, cells, cond, rhs)
        ),
        [far_memory] * 4,
        [
            pltpu.SMEM((8, 8), jnp.int32),
            pltpu.VMEM((8, 256), jnp.int32),
            pltpu.VMEM(whole, F32),
            pltpu.VMEM(whole, F32),
            pltpu.SemaphoreType.DMA((4,)),
        ],
    )
    beyond = [(i, i + 1) for i in range(1, size - 1, 2)]
    far_in = lax.ppermute(far, "gx", beyond + [(j, i) for i, j in beyond])
    near_in = lax.ppermute(near, "gx", [(i, i ^ 1) for i in range(size)])
    (donors,) = call(donor_kernel, "donor", [(8, 256)], (base, frac, smoothed), [vector] * 3)
    (sent,) = call(
        pack_kernel, "pack", [(8 * CHUNK, 128)], (donors, smoothed, cond, far_in, near_in),
        [vector] * 5,
    )
    arrived = lax.all_to_all(
        sent.reshape(8 * CHUNK, 1, 128), "gy", split_axis=0, concat_axis=0, tiled=True,
        axis_index_groups=[[(i + TURN) % 8 for i in range(8)]],
    ).reshape(8 * CHUNK, 128)
    partial, coarse = call(
        residual_kernel, "residual", [whole, (64, 2, 128)],
        (marked, arrived, smoothed, count, rhs, cond, far_in, near_in), [vector] * 8,
    )
    groups = [
        [
            (start + (i ^ int(side_of(start)))) * 8 + (j + LATER) % 8
            for i in range(ROW)
            for j in range(8)
        ]
        for start in range(0, size, ROW)
    ]
    gathered = lax.all_to_all(
        coarse, ("gx", "gy"), split_axis=0, concat_axis=0, tiled=True, axis_index_groups=groups
    ).reshape(128, 128)
    passed, token = call(
        pass_kernel, "pass", [(48, 128), (8, 128)], (gathered,), [vector]
    )
    step = [(i, i + ROW) if i % ROW < ROW // 2 else (i, i - ROW) for i in range(size)]
    extra = lax.ppermute(passed, "gx", [(i, j) for i, j in step if 0 <= j < size])
    (residual,) = call(store_kernel, "store", [whole], (token, partial), [vector] * 2)
    (pressure,) = call(
        coarse_kernel, "coarse", [whole],
        (gathered, extra, smoothed), [vector] * 3,
    )
    return pressure.reshape(shape), residual.reshape(shape)


def solution(mesh):
    return jax.shard_map(
        local,
        mesh=mesh,
        in_specs=(
            P(None, "gx", "gy", None),
            P(None, "gx", "gy", None),
            P("gx", None, None),
            P("gx", "gy", None, None),
            P(None, "gx", "gy", None, None),
            P("gx", "gy", None, None),
        ),
        out_specs=(P(None, "gx", "gy", None), P(None, "gx", "gy", None)),
        check_vma=False,
    )
```

```python
import functools

import jax
import jax.numpy as jnp
from jax import lax
from jax.experimental import pallas as pl
from jax.experimental.pallas import tpu as pltpu
from jax.sharding import PartitionSpec as P

BLOCK = 128
ROW = 8
TURN = 5
CHUNK = 26
LATER = 4


def side_of(along):
    return 4 * (along >= ROW)


F32 = jnp.float32
BF16 = jnp.bfloat16
damping = 0.8
penalty_weight = 2.0
coarse_scale = 0.0625
stencil_weight_sum = 44.0 / 3.0
half_weight_sum = 22.0 / 3.0
MEMORY = 32 * 1024 * 1024


def iota(shape, axis):
    return lax.broadcasted_iota(jnp.int32, shape, axis)


def place():
    along = lax.axis_index("gx")
    return along, lax.axis_index("gy"), lax.rem(along, 2) == 0


def parts(value, count):
    cuts = []
    for index in range(count):
        cut = value.astype(BF16)
        cuts.append(cut)
        if index + 1 < count:
            value = value - cut.astype(F32)
    return cuts


def one_hots(cells):
    rows = cells.shape[1]
    low = iota((128, rows), 0) == (cells & 127)
    return iota((64, rows), 0) == (cells >> 7), low.astype(F32).astype(BF16)


def exact_product(value, table):
    rows = value.shape[0]
    cuts = jnp.dot(
        jnp.concatenate(parts(value, 3), axis=0), table.astype(F32).astype(BF16),
        preferred_element_type=F32,
    )
    return cuts[0:rows] + cuts[rows : 2 * rows] + cuts[2 * rows : 3 * rows]


def contract_rows(left, right):
    return lax.dot_general(left, right, (((1,), (1,)), ((), ())), preferred_element_type=F32)


def front_kernel(
    counts_in, cells_in, cond_in, rhs_in, smoothed, count, near, far, marked,
    counts, cells, cond, rhs, sems,
):
    _, own, first = place()
    pairs = ((counts_in, counts), (cells_in, cells), (cond_in, cond), (rhs_in, rhs))
    copies = [
        pltpu.make_async_copy(source, target, sems.at[i]) for i, (source, target) in enumerate(pairs)
    ]
    for copy in copies:
        copy.start()
    copies[0].wait()
    copies[1].wait()
    mine = jnp.where(iota((8, 8), 1) == own, counts[...], 0)
    limit = jnp.sum(mine, axis=1, keepdims=True) * BLOCK
    valid = jnp.where(iota((8, 256), 1) < limit, cells[...], -BLOCK)
    marked[...] = valid
    total = jnp.zeros((64, 128), F32)
    for b in range(8):
        row = valid[b : b + 1, :]
        high, low = one_hots(row)
        total = total + contract_rows(high.astype(F32).astype(BF16), low)
    count[...] = total
    copies[2].wait()
    copies[3].wait()
    field = damping * rhs[...] / (stencil_weight_sum * cond[...] + penalty_weight * total)
    smoothed[...] = field
    for f, ref in ((0, smoothed), (16, cond)):
        for grid in range(2):
            low_x = ref[grid * 32 : grid * 32 + 8, :]
            high_x = ref[grid * 32 + 24 : grid * 32 + 32, :]
            at = slice(f + grid * 8, f + grid * 8 + 8)
            near[at, :] = jnp.where(first, high_x, low_x)
            far[at, :] = jnp.where(first, low_x, high_x)


def donor_kernel(base, frac, smoothed, donors):
    field = smoothed[...]
    high = field.astype(BF16).astype(F32)
    stacked = jnp.concatenate([high, field - high, high], axis=0)
    columns = stacked.T.astype(BF16)
    q = base[...]
    grid = (q >= 2667).astype(jnp.int32)
    q = q - grid * 2667
    x = (q >= 889).astype(jnp.int32) + (q >= 1778).astype(jnp.int32)
    q = q - x * 889
    y = jnp.zeros_like(q)
    for step in range(1, 7):
        y = y + (q >= step * 127).astype(jnp.int32)
    z = q - y * 127
    plane = grid * 4 + x
    eight = iota((8, 256), 0)
    wide = iota((128, 256), 0)
    for d in range(8):
        row = slice(d, d + 1)
        frac_x, frac_y, frac_z = frac[0, row, :], frac[1, row, :], frac[2, row, :]
        at_x, at_y, at_z = plane[row], y[row], z[row]
        weight_x = jnp.where(eight == at_x, 1.0 - frac_x, jnp.where(eight == at_x + 1, frac_x, 0.0))
        weight_y = jnp.where(eight == at_y, 1.0 - frac_y, jnp.where(eight == at_y + 1, frac_y, 0.0))
        weight_z = jnp.where(wide == at_z, 1.0 - frac_z, jnp.where(wide == at_z + 1, frac_z, 0.0))
        weight = jnp.concatenate([weight_x[p : p + 1] * weight_y for p in range(8)], axis=0)
        upper, lower = parts(weight, 2)
        mixed = jnp.dot(
            columns, jnp.concatenate([upper, upper, lower], axis=0), preferred_element_type=F32
        )
        donors[row, :] = jnp.sum(mixed * weight_z, axis=0, keepdims=True)


def pack_kernel(donors, smoothed, cond, far, near, sent):
    _, own, first = place()
    faces = []
    for y in (0, 7):
        near_rows = near[pl.ds(y, 4, stride=8), :]
        far_rows = far[pl.ds(y, 4, stride=8), :]
        faces.append(
            (
                smoothed[pl.ds(y, 8, stride=8), :],
                cond[pl.ds(y, 8, stride=8), :],
                jnp.where(first, far_rows, near_rows),
                jnp.where(first, near_rows, far_rows),
            )
        )
    for d in range(8):
        start = (d - TURN) % 8 * CHUNK
        for f, (row, count) in enumerate(((0, 8), (8, 8), (16, 4), (20, 4))):
            sent[start + row : start + row + count, :] = jnp.where(
                d > own, faces[1][f], faces[0][f]
            )
        sent[start + 24 : start + 25, :] = donors[d : d + 1, 0:128]
        sent[start + 25 : start + 26, :] = donors[d : d + 1, 128:256]


def residual_kernel(
    cells, arrived, smoothed, count, rhs, cond, far, near, partial, coarse
):
    _, own, first = place()
    total = jnp.zeros((128, 128), F32)
    for b in range(8):
        high, low = one_hots(cells[b : b + 1, :])
        values = jnp.concatenate([
                arrived[(b - TURN) % 8 * CHUNK + row : (b - TURN) % 8 * CHUNK + row + 1, :]
                for row in (24, 25)
            ], axis=1)
        left = jnp.concatenate(
            [jnp.where(high, cut.astype(F32), 0.0).astype(BF16) for cut in parts(values, 2)], axis=0
        )
        total = total + contract_rows(left, low)
    total = total[0:64] + total[64:128]

    below = jnp.where(own > 0, arrived[pl.ds(((own + 7 - TURN) & 7) * CHUNK, 24), :], 0.0)
    above = jnp.where(own < 7, arrived[pl.ds(((own + 9 - TURN) & 7) * CHUNK, 24), :], 0.0)
    lanes = iota((8, 128), 1)
    rows = iota((8, 128), 0)
    keep_up = lanes < 127
    keep_down = lanes > 0

    def shift_z(value):
        return jnp.where(keep_down, pltpu.roll(value, 1, 1), 0.0) + jnp.where(
            keep_up, pltpu.roll(value, 127, 1), 0.0
        )

    def shift_y(value, lower, upper):
        down = jnp.where(rows > 0, pltpu.roll(value, 1, 0), lower)
        up = jnp.where(rows < 7, pltpu.roll(value, 7, 0), upper)
        return down + up

    pooled = []
    for grid in range(2):
        fields = []
        for f, ref in ((0, smoothed), (1, cond)):
            at = slice((2 * f + grid) * 8, (2 * f + grid) * 8 + 8)
            near_plane, far_plane = near[at, :], far[at, :]
            left = jnp.where(first, far_plane, near_plane)
            right = jnp.where(first, near_plane, far_plane)
            start = grid * 32
            planes = [left] + [ref[start + x * 8 : start + x * 8 + 8, :] for x in range(4)] + [right]
            at = [16 + 2 * f + grid] + [8 * f + grid * 4 + x for x in range(4)] + [20 + 2 * f + grid]
            lower = [below[row : row + 1, :] for row in at]
            upper = [above[row : row + 1, :] for row in at]
            fields.append((planes, lower, upper))
        fields.append(tuple([v * c for v, c in zip(*pair)] for pair in zip(*fields)))
        sums = []
        for planes, lower, upper in fields:
            inner, outer = [], []
            for plane, low_row, high_row in zip(planes, lower, upper):
                beside_z = shift_z(plane)
                beside_y = shift_y(plane, low_row, high_row)
                both = shift_z(beside_y)
                edge = beside_z + beside_y
                inner.append(0.5 * edge + 0.25 * both)
                outer.append(0.5 * plane + 0.25 * edge + (1.0 / 6.0) * both)
            sums.append([inner[i] + outer[i - 1] + outer[i + 1] for i in range(1, 5)])
        summed = jnp.zeros((8, 128), F32)
        for x in range(4):
            at = slice(grid * 32 + x * 8, grid * 32 + x * 8 + 8)
            v, c = smoothed[at, :], cond[at, :]
            applied = v * (half_weight_sum * c + sums[1][x]) - c * sums[0][x] - sums[2][x]
            value = rhs[at, :] - applied - penalty_weight * (count[at, :] * v - total[at])
            partial[at, :] = value
            summed = summed + value
        pooled.append(summed)
    for grid in range(2):
        start = grid * 32
        pooled.append(sum(cond[start + x * 8 : start + x * 8 + 8, :] for x in range(4)))

    pool = iota((128, 128), 0) // 4 == iota((128, 128), 1) % 32
    means = exact_product(jnp.concatenate(pooled, axis=0), pool) * (1.0 / 64.0)
    own_part = iota((16, 128), 0) // 4 == iota((16, 128), 1) // 32
    lines = [
        jnp.sum(jnp.where(own_part, means[f * 16 : f * 16 + 16], 0.0), axis=0, keepdims=True)
        for f in range(2)
    ]
    coarse[...] = jnp.broadcast_to(jnp.concatenate(lines, axis=0)[None], (64, 2, 128))


def pass_kernel(gathered, passed, token):
    along, _, _ = place()
    low_half = lax.rem(along, ROW) < ROW // 2
    start = (jnp.where(low_half, ROW // 2, 0) ^ side_of(along)) & 4
    start = start * 16 + jnp.where(low_half, 16, 0)
    passed[...] = gathered[pl.ds(pl.multiple_of(start, 16), 48), :]
    token[...] = gathered[0:8, :]


def store_kernel(token, partial, residual):
    residual[...] = partial[...]


def coarse_kernel(gathered, extra, smoothed, pressure):
    along, own, _ = place()
    column, side = lax.rem(along, ROW), side_of(along)
    skip = jnp.where(column < ROW // 2, 1, 0)
    lanes = iota((8, 128), 1)
    rows = (iota((8, 128), 0) + LATER) & 7
    low_z = lanes % 32 > 0
    high_z = lanes % 32 < 31
    first_y = lanes % 64 < 32

    def shift_z(value):
        return jnp.where(low_z, pltpu.roll(value, 1, 1), 0.0) + jnp.where(
            high_z, pltpu.roll(value, 127, 1), 0.0
        )

    def shift_y(value):
        ahead = pltpu.roll(value, 96, 1)
        behind = pltpu.roll(value, 32, 1)
        within = jnp.where(first_y, ahead, behind)
        from_below = jnp.where(rows > 0, pltpu.roll(ahead, 1, 0), 0.0)
        from_above = jnp.where(rows < 7, pltpu.roll(behind, 7, 0), 0.0)
        return within + jnp.where(first_y, from_below, from_above)

    def neighbour_sums(fields):
        sums = []
        for i in range(1, len(fields) - 1):
            field, beside = fields[i], fields[i - 1] + fields[i + 1]
            edge = 0.5 * field + 0.25 * beside
            corner = 0.25 * field + (1.0 / 6.0) * beside
            sums.append(0.5 * beside + shift_y(edge) + shift_z(edge + shift_y(corner)))
        return sums

    rhs, cond = [], []
    for slot in range(7):
        at = column + slot - 3
        inside = jnp.logical_and(at >= 0, at < ROW)
        here = pl.multiple_of((jnp.clip(at, 0, ROW - 1) ^ side) * 16, 16)
        there = pl.multiple_of(jnp.clip((at & 3) - skip, 0, 2) * 16, 16)
        for f, out in ((0, rhs), (1, cond)):
            out.append(
                jnp.where(inside, gathered[pl.ds(here + f, 8, stride=2), :],
                    extra[pl.ds(there + f, 8, stride=2), :],)
            )
    scale = [
        jnp.where(c > 0.0, damping / (stencil_weight_sum * coarse_scale * jnp.where(c > 0.0, c, 1.0)), 0.0)
        for c in cond
    ]
    value = [r * s for r, s in zip(rhs, scale)]
    own_sum = [
        half_weight_sum * c + s for c, s in zip(cond[1:-1], neighbour_sums(cond))
    ]
    for sweep in range(3):
        around = neighbour_sums(value)
        around_both = neighbour_sums([v * c for v, c in zip(value, cond)])
        value, cond, rhs, scale = value[1:-1], cond[1:-1], rhs[1:-1], scale[1:-1]
        value = [
            v + s * (r - coarse_scale * (v * o - c * a - b))
            for v, s, r, o, c, a, b in zip(value, scale, rhs, own_sum, cond, around, around_both)
        ]
        own_sum = own_sum[1:-1]
    mine = jnp.sum(jnp.where(rows == own, value[0], 0.0), axis=0, keepdims=True)
    spread = jnp.where(iota((16, 128), 0) // 4 == iota((16, 128), 1) // 32, mine, 0.0)
    expand = iota((128, 128), 0) % 32 == iota((128, 128), 1) // 4
    fine = exact_product(spread, expand)
    for grid in range(2):
        for x in range(4):
            at = slice(grid * 32 + x * 8, grid * 32 + x * 8 + 8)
            pressure[at, :] = smoothed[at, :] + fine[grid * 8 : grid * 8 + 8]


def call(kernel, name, outs, operands, spaces, scratch=()):
    return pl.pallas_call(
        kernel,
        out_shape=[
            jax.ShapeDtypeStruct(*(out if isinstance(out[0], tuple) else (out, F32))) for out in outs
        ],
        in_specs=[pl.BlockSpec(memory_space=space) for space in spaces],
        out_specs=[pl.BlockSpec(memory_space=pltpu.VMEM)] * len(outs),
        scratch_shapes=scratch,
        compiler_params=pltpu.CompilerParams(vmem_limit_bytes=MEMORY),
        cost_estimate=pl.CostEstimate(flops=1000000, bytes_accessed=200000, transcendentals=0),
        name=name,
    )(*operands)


def local(pressure_rhs, conductivity, block_counts, donor_base, donor_frac, receptor_cells):
    shape = pressure_rhs.shape
    size = lax.axis_size("gx")
    rhs = pressure_rhs.reshape(64, 128)
    cond = conductivity.reshape(64, 128)
    counts = block_counts[0]
    cells = receptor_cells[0, 0]
    base = donor_base[0, 0]
    frac = donor_frac[:, 0, 0]
    vector, far_memory = pltpu.VMEM, pltpu.HBM
    whole = (64, 128)
    smoothed, count, near, far, marked = call(
        front_kernel, "front",
        [whole, whole, (32, 128), (32, 128), ((8, 256), jnp.int32)],
        tuple(
            pltpu.with_memory_space_constraint(value, far_memory)
            for value in (counts, cells, cond, rhs)
        ),
        [far_memory] * 4,
        [
            pltpu.VMEM((8, 8), jnp.int32),
            pltpu.VMEM((8, 256), jnp.int32),
            pltpu.VMEM(whole, F32),
            pltpu.VMEM(whole, F32),
            pltpu.SemaphoreType.DMA((4,)),
        ],
    )
    beyond = [(i, i + 1) for i in range(1, size - 1, 2)]
    far_in = lax.ppermute(far, "gx", beyond + [(j, i) for i, j in beyond])
    near_in = lax.ppermute(near, "gx", [(i, i ^ 1) for i in range(size)])
    (donors,) = call(donor_kernel, "donor", [(8, 256)], (base, frac, smoothed), [vector] * 3)
    (sent,) = call(
        pack_kernel, "pack", [(8 * CHUNK, 128)], (donors, smoothed, cond, far_in, near_in),
        [vector] * 5,
    )
    arrived = lax.all_to_all(
        sent.reshape(8 * CHUNK, 1, 128), "gy", split_axis=0, concat_axis=0, tiled=True,
        axis_index_groups=[[(i + TURN) % 8 for i in range(8)]],
    ).reshape(8 * CHUNK, 128)
    partial, coarse = call(
        residual_kernel, "residual", [whole, (64, 2, 128)],
        (marked, arrived, smoothed, count, rhs, cond, far_in, near_in), [vector] * 8,
    )
    groups = [
        [
            (start + (i ^ int(side_of(start)))) * 8 + (j + LATER) % 8
            for i in range(ROW)
            for j in range(8)
        ]
        for start in range(0, size, ROW)
    ]
    gathered = lax.all_to_all(
        coarse, ("gx", "gy"), split_axis=0, concat_axis=0, tiled=True, axis_index_groups=groups
    ).reshape(128, 128)
    passed, token = call(
        pass_kernel, "pass", [(48, 128), (8, 128)], (gathered,), [vector]
    )
    step = [(i, i + ROW) if i % ROW < ROW // 2 else (i, i - ROW) for i in range(size)]
    extra = lax.ppermute(passed, "gx", [(i, j) for i, j in step if 0 <= j < size])
    (residual,) = call(store_kernel, "store", [whole], (token, partial), [vector] * 2)
    (pressure,) = call(
        coarse_kernel, "coarse", [whole],
        (gathered, extra, smoothed), [vector] * 3,
    )
    return pressure.reshape(shape), residual.reshape(shape)


def solution(mesh):
    return jax.shard_map(
        local,
        mesh=mesh,
        in_specs=(
            P(None, "gx", "gy", None),
            P(None, "gx", "gy", None),
            P("gx", None, None),
            P("gx", "gy", None, None),
            P(None, "gx", "gy", None, None),
            P("gx", "gy", None, None),
        ),
        out_specs=(P(None, "gx", "gy", None), P(None, "gx", "gy", None)),
        check_vma=False,
    )
```

```python
import functools

import jax
import jax.numpy as jnp
from jax import lax
from jax.experimental import pallas as pl
from jax.experimental.pallas import tpu as pltpu
from jax.sharding import PartitionSpec as P

BLOCK = 128
ROW = 8
TURN = 5
CHUNK = 26
LATER = 4


def side_of(along):
    return 4 * (along >= ROW)


F32 = jnp.float32
BF16 = jnp.bfloat16
damping = 0.8
penalty_weight = 2.0
coarse_scale = 0.0625
stencil_weight_sum = 44.0 / 3.0
half_weight_sum = 22.0 / 3.0
MEMORY = 32 * 1024 * 1024


def iota(shape, axis):
    return lax.broadcasted_iota(jnp.int32, shape, axis)


def place():
    along = lax.axis_index("gx")
    return along, lax.axis_index("gy"), lax.rem(along, 2) == 0


def parts(value, count):
    cuts = []
    for index in range(count):
        cut = value.astype(BF16)
        cuts.append(cut)
        if index + 1 < count:
            value = value - cut.astype(F32)
    return cuts


def one_hots(cells):
    rows = cells.shape[1]
    low = iota((128, rows), 0) == (cells & 127)
    return iota((64, rows), 0) == (cells >> 7), low.astype(F32).astype(BF16)


def exact_product(value, table):
    rows = value.shape[0]
    cuts = jnp.dot(
        jnp.concatenate(parts(value, 3), axis=0), table.astype(F32).astype(BF16),
        preferred_element_type=F32,
    )
    return cuts[0:rows] + cuts[rows : 2 * rows] + cuts[2 * rows : 3 * rows]


def contract_rows(left, right):
    return lax.dot_general(left, right, (((1,), (1,)), ((), ())), preferred_element_type=F32)


def front_kernel(
    counts_in, cells_in, cond_in, rhs_in, smoothed, count, near, far, marked,
    counts, cells, cond, rhs, sems,
):
    _, own, first = place()
    pairs = ((counts_in, counts), (cells_in, cells), (cond_in, cond), (rhs_in, rhs))
    copies = [
        pltpu.make_async_copy(source, target, sems.at[i]) for i, (source, target) in enumerate(pairs)
    ]
    for copy in copies:
        copy.start()
    copies[0].wait()
    copies[1].wait()
    mine = jnp.where(iota((8, 8), 1) == own, counts[...], 0)
    limit = jnp.sum(mine, axis=1, keepdims=True) * BLOCK
    valid = jnp.where(iota((8, 256), 1) < limit, cells[...], -BLOCK)
    marked[...] = valid
    total = jnp.zeros((64, 128), F32)
    for b in range(8):
        row = valid[b : b + 1, :]
        high, low = one_hots(row)
        total = total + contract_rows(high.astype(F32).astype(BF16), low)
    count[...] = total
    copies[2].wait()
    copies[3].wait()
    field = damping * rhs[...] / (stencil_weight_sum * cond[...] + penalty_weight * total)
    smoothed[...] = field
    for f, ref in ((0, smoothed), (16, cond)):
        for grid in range(2):
            low_x = ref[grid * 32 : grid * 32 + 8, :]
            high_x = ref[grid * 32 + 24 : grid * 32 + 32, :]
            at = slice(f + grid * 8, f + grid * 8 + 8)
            near[at, :] = jnp.where(first, high_x, low_x)
            far[at, :] = jnp.where(first, low_x, high_x)


def donor_kernel(base, frac, smoothed, donors):
    field = smoothed[...]
    high = field.astype(BF16).astype(F32)
    stacked = jnp.concatenate([high, field - high, high], axis=0)
    columns = stacked.T.astype(BF16)
    q = base[...]
    grid = (q >= 2667).astype(jnp.int32)
    q = q - grid * 2667
    x = (q >= 889).astype(jnp.int32) + (q >= 1778).astype(jnp.int32)
    q = q - x * 889
    y = jnp.zeros_like(q)
    for step in range(1, 7):
        y = y + (q >= step * 127).astype(jnp.int32)
    z = q - y * 127
    plane = grid * 4 + x
    eight = iota((8, 256), 0)
    wide = iota((128, 256), 0)
    for d in range(8):
        row = slice(d, d + 1)
        frac_x, frac_y, frac_z = frac[0, row, :], frac[1, row, :], frac[2, row, :]
        at_x, at_y, at_z = plane[row], y[row], z[row]
        weight_x = jnp.where(eight == at_x, 1.0 - frac_x, jnp.where(eight == at_x + 1, frac_x, 0.0))
        weight_y = jnp.where(eight == at_y, 1.0 - frac_y, jnp.where(eight == at_y + 1, frac_y, 0.0))
        weight_z = jnp.where(wide == at_z, 1.0 - frac_z, jnp.where(wide == at_z + 1, frac_z, 0.0))
        weight = jnp.concatenate([weight_x[p : p + 1] * weight_y for p in range(8)], axis=0)
        upper, lower = parts(weight, 2)
        mixed = jnp.dot(
            columns, jnp.concatenate([upper, upper, lower], axis=0), preferred_element_type=F32
        )
        donors[row, :] = jnp.sum(mixed * weight_z, axis=0, keepdims=True)


def pack_kernel(donors, smoothed, cond, far, near, sent):
    _, own, first = place()
    faces = []
    for y in (0, 7):
        near_rows = near[pl.ds(y, 4, stride=8), :]
        far_rows = far[pl.ds(y, 4, stride=8), :]
        faces.append(
            (
                smoothed[pl.ds(y, 8, stride=8), :],
                cond[pl.ds(y, 8, stride=8), :],
                jnp.where(first, far_rows, near_rows),
                jnp.where(first, near_rows, far_rows),
            )
        )
    for d in range(8):
        start = (d - TURN) % 8 * CHUNK
        for f, (row, count) in enumerate(((0, 8), (8, 8), (16, 4), (20, 4))):
            sent[start + row : start + row + count, :] = jnp.where(
                d > own, faces[1][f], faces[0][f]
            )
        sent[start + 24 : start + 25, :] = donors[d : d + 1, 0:128]
        sent[start + 25 : start + 26, :] = donors[d : d + 1, 128:256]


def residual_kernel(
    cells, arrived, smoothed, count, rhs, cond, far, near, partial, coarse
):
    _, own, first = place()
    total = jnp.zeros((128, 128), F32)
    for b in range(8):
        high, low = one_hots(cells[b : b + 1, :])
        values = jnp.concatenate([
                arrived[(b - TURN) % 8 * CHUNK + row : (b - TURN) % 8 * CHUNK + row + 1, :]
                for row in (24, 25)
            ], axis=1)
        left = jnp.concatenate(
            [jnp.where(high, cut.astype(F32), 0.0).astype(BF16) for cut in parts(values, 2)], axis=0
        )
        total = total + contract_rows(left, low)
    total = total[0:64] + total[64:128]

    below = jnp.where(own > 0, arrived[pl.ds(((own + 7 - TURN) & 7) * CHUNK, 24), :], 0.0)
    above = jnp.where(own < 7, arrived[pl.ds(((own + 9 - TURN) & 7) * CHUNK, 24), :], 0.0)
    lanes = iota((8, 128), 1)
    rows = iota((8, 128), 0)
    keep_up = lanes < 127
    keep_down = lanes > 0

    def shift_z(value):
        return jnp.where(keep_down, pltpu.roll(value, 1, 1), 0.0) + jnp.where(
            keep_up, pltpu.roll(value, 127, 1), 0.0
        )

    def shift_y(value, lower, upper):
        down = jnp.where(rows > 0, pltpu.roll(value, 1, 0), lower)
        up = jnp.where(rows < 7, pltpu.roll(value, 7, 0), upper)
        return down + up

    pooled = []
    for grid in range(2):
        fields = []
        for f, ref in ((0, smoothed), (1, cond)):
            at = slice((2 * f + grid) * 8, (2 * f + grid) * 8 + 8)
            near_plane, far_plane = near[at, :], far[at, :]
            left = jnp.where(first, far_plane, near_plane)
            right = jnp.where(first, near_plane, far_plane)
            start = grid * 32
            planes = [left] + [ref[start + x * 8 : start + x * 8 + 8, :] for x in range(4)] + [right]
            at = [16 + 2 * f + grid] + [8 * f + grid * 4 + x for x in range(4)] + [20 + 2 * f + grid]
            lower = [below[row : row + 1, :] for row in at]
            upper = [above[row : row + 1, :] for row in at]
            fields.append((planes, lower, upper))
        fields.append(tuple([v * c for v, c in zip(*pair)] for pair in zip(*fields)))
        sums = []
        for planes, lower, upper in fields:
            inner, outer = [], []
            for plane, low_row, high_row in zip(planes, lower, upper):
                beside_z = shift_z(plane)
                beside_y = shift_y(plane, low_row, high_row)
                both = shift_z(beside_y)
                edge = beside_z + beside_y
                inner.append(0.5 * edge + 0.25 * both)
                outer.append(0.5 * plane + 0.25 * edge + (1.0 / 6.0) * both)
            sums.append([inner[i] + outer[i - 1] + outer[i + 1] for i in range(1, 5)])
        summed = jnp.zeros((8, 128), F32)
        for x in range(4):
            at = slice(grid * 32 + x * 8, grid * 32 + x * 8 + 8)
            v, c = smoothed[at, :], cond[at, :]
            applied = v * (half_weight_sum * c + sums[1][x]) - c * sums[0][x] - sums[2][x]
            value = rhs[at, :] - applied - penalty_weight * (count[at, :] * v - total[at])
            partial[at, :] = value
            summed = summed + value
        pooled.append(summed)
    for grid in range(2):
        start = grid * 32
        pooled.append(sum(cond[start + x * 8 : start + x * 8 + 8, :] for x in range(4)))

    pool = iota((128, 128), 0) // 4 == iota((128, 128), 1) % 32
    means = exact_product(jnp.concatenate(pooled, axis=0), pool) * (1.0 / 64.0)
    own_part = iota((16, 128), 0) // 4 == iota((16, 128), 1) // 32
    lines = [
        jnp.sum(jnp.where(own_part, means[f * 16 : f * 16 + 16], 0.0), axis=0, keepdims=True)
        for f in range(2)
    ]
    coarse[...] = jnp.broadcast_to(jnp.concatenate(lines, axis=0)[None], (64, 2, 128))


def pass_kernel(gathered, passed, token):
    along, own, _ = place()
    low_half = lax.rem(along, ROW) < ROW // 2
    start = ((jnp.where(low_half, ROW // 2, 0) ^ side_of(along)) & 4) + jnp.where(low_half, 1, 0)
    for r in range(5):
        line = (own + r + 6 - LATER) & 7
        passed[r * 6 : r * 6 + 6, :] = gathered[pl.ds(line * 16 + start * 2, 6), :]
    token[...] = gathered[0:8, :]


def store_kernel(token, partial, residual):
    residual[...] = partial[...]


def coarse_kernel(gathered, extra_in, smoothed, pressure, extra):
    along, own, _ = place()
    extra[...] = jnp.zeros((48, 128), F32)
    for r in range(5):
        extra[pl.ds(((own + r + 6 - LATER) & 7) * 6, 6), :] = extra_in[r * 6 : r * 6 + 6, :]
    column, side = lax.rem(along, ROW), side_of(along)
    skip = jnp.where(column < ROW // 2, 1, 0)
    lanes = iota((8, 128), 1)
    rows = (iota((8, 128), 0) + LATER) & 7
    low_z = lanes % 32 > 0
    high_z = lanes % 32 < 31
    first_y = lanes % 64 < 32

    def shift_z(value):
        return jnp.where(low_z, pltpu.roll(value, 1, 1), 0.0) + jnp.where(
            high_z, pltpu.roll(value, 127, 1), 0.0
        )

    def shift_y(value):
        ahead = pltpu.roll(value, 96, 1)
        behind = pltpu.roll(value, 32, 1)
        within = jnp.where(first_y, ahead, behind)
        from_below = jnp.where(rows > 0, pltpu.roll(ahead, 1, 0), 0.0)
        from_above = jnp.where(rows < 7, pltpu.roll(behind, 7, 0), 0.0)
        return within + jnp.where(first_y, from_below, from_above)

    def neighbour_sums(fields):
        sums = []
        for i in range(1, len(fields) - 1):
            field, beside = fields[i], fields[i - 1] + fields[i + 1]
            edge = 0.5 * field + 0.25 * beside
            corner = 0.25 * field + (1.0 / 6.0) * beside
            sums.append(0.5 * beside + shift_y(edge) + shift_z(edge + shift_y(corner)))
        return sums

    rhs, cond = [], []
    for slot in range(7):
        at = column + slot - 3
        inside = jnp.logical_and(at >= 0, at < ROW)
        here = (jnp.clip(at, 0, ROW - 1) ^ side) * 2
        there = jnp.clip((at & 3) - skip, 0, 2) * 2
        for f, out in ((0, rhs), (1, cond)):
            out.append(
                jnp.where(inside, gathered[pl.ds(here + f, 8, stride=16), :],
                    extra[pl.ds(there + f, 8, stride=6), :],)
            )
    scale = [
        jnp.where(c > 0.0, damping / (stencil_weight_sum * coarse_scale * jnp.where(c > 0.0, c, 1.0)), 0.0)
        for c in cond
    ]
    value = [r * s for r, s in zip(rhs, scale)]
    own_sum = [
        half_weight_sum * c + s for c, s in zip(cond[1:-1], neighbour_sums(cond))
    ]
    for sweep in range(3):
        around = neighbour_sums(value)
        around_both = neighbour_sums([v * c for v, c in zip(value, cond)])
        value, cond, rhs, scale = value[1:-1], cond[1:-1], rhs[1:-1], scale[1:-1]
        value = [
            v + s * (r - coarse_scale * (v * o - c * a - b))
            for v, s, r, o, c, a, b in zip(value, scale, rhs, own_sum, cond, around, around_both)
        ]
        own_sum = own_sum[1:-1]
    mine = jnp.sum(jnp.where(rows == own, value[0], 0.0), axis=0, keepdims=True)
    spread = jnp.where(iota((16, 128), 0) // 4 == iota((16, 128), 1) // 32, mine, 0.0)
    expand = iota((128, 128), 0) % 32 == iota((128, 128), 1) // 4
    fine = exact_product(spread, expand)
    for grid in range(2):
        for x in range(4):
            at = slice(grid * 32 + x * 8, grid * 32 + x * 8 + 8)
            pressure[at, :] = smoothed[at, :] + fine[grid * 8 : grid * 8 + 8]


def call(kernel, name, outs, operands, spaces, scratch=()):
    return pl.pallas_call(
        kernel,
        out_shape=[
            jax.ShapeDtypeStruct(*(out if isinstance(out[0], tuple) else (out, F32))) for out in outs
        ],
        in_specs=[pl.BlockSpec(memory_space=space) for space in spaces],
        out_specs=[pl.BlockSpec(memory_space=pltpu.VMEM)] * len(outs),
        scratch_shapes=scratch,
        compiler_params=pltpu.CompilerParams(vmem_limit_bytes=MEMORY),
        cost_estimate=pl.CostEstimate(flops=1000000, bytes_accessed=200000, transcendentals=0),
        name=name,
    )(*operands)


def local(pressure_rhs, conductivity, block_counts, donor_base, donor_frac, receptor_cells):
    shape = pressure_rhs.shape
    size = lax.axis_size("gx")
    rhs = pressure_rhs.reshape(64, 128)
    cond = conductivity.reshape(64, 128)
    counts = block_counts[0]
    cells = receptor_cells[0, 0]
    base = donor_base[0, 0]
    frac = donor_frac[:, 0, 0]
    vector, far_memory = pltpu.VMEM, pltpu.HBM
    whole = (64, 128)
    smoothed, count, near, far, marked = call(
        front_kernel, "front",
        [whole, whole, (32, 128), (32, 128), ((8, 256), jnp.int32)],
        tuple(
            pltpu.with_memory_space_constraint(value, far_memory)
            for value in (counts, cells, cond, rhs)
        ),
        [far_memory] * 4,
        [
            pltpu.VMEM((8, 8), jnp.int32),
            pltpu.VMEM((8, 256), jnp.int32),
            pltpu.VMEM(whole, F32),
            pltpu.VMEM(whole, F32),
            pltpu.SemaphoreType.DMA((4,)),
        ],
    )
    beyond = [(i, i + 1) for i in range(1, size - 1, 2)]
    far_in = lax.ppermute(far, "gx", beyond + [(j, i) for i, j in beyond])
    near_in = lax.ppermute(near, "gx", [(i, i ^ 1) for i in range(size)])
    (donors,) = call(donor_kernel, "donor", [(8, 256)], (base, frac, smoothed), [vector] * 3)
    (sent,) = call(
        pack_kernel, "pack", [(8 * CHUNK, 128)], (donors, smoothed, cond, far_in, near_in),
        [vector] * 5,
    )
    arrived = lax.all_to_all(
        sent.reshape(8 * CHUNK, 1, 128), "gy", split_axis=0, concat_axis=0, tiled=True,
        axis_index_groups=[[(i + TURN) % 8 for i in range(8)]],
    ).reshape(8 * CHUNK, 128)
    partial, coarse = call(
        residual_kernel, "residual", [whole, (64, 2, 128)],
        (marked, arrived, smoothed, count, rhs, cond, far_in, near_in), [vector] * 8,
    )
    groups = [
        [
            (start + (i ^ int(side_of(start)))) * 8 + (j + LATER) % 8
            for j in range(8)
            for i in range(ROW)
        ]
        for start in range(0, size, ROW)
    ]
    gathered = lax.all_to_all(
        coarse, ("gx", "gy"), split_axis=0, concat_axis=0, tiled=True, axis_index_groups=groups
    ).reshape(128, 128)
    passed, token = call(
        pass_kernel, "pass", [(30, 128), (8, 128)], (gathered,), [vector]
    )
    step = [(i, i + ROW) if i % ROW < ROW // 2 else (i, i - ROW) for i in range(size)]
    extra = lax.ppermute(passed, "gx", [(i, j) for i, j in step if 0 <= j < size])
    (residual,) = call(store_kernel, "store", [whole], (token, partial), [vector] * 2)
    (pressure,) = call(
        coarse_kernel, "coarse", [whole],
        (gathered, extra, smoothed), [vector] * 3, [pltpu.VMEM((48, 128), F32)],
    )
    return pressure.reshape(shape), residual.reshape(shape)


def solution(mesh):
    return jax.shard_map(
        local,
        mesh=mesh,
        in_specs=(
            P(None, "gx", "gy", None),
            P(None, "gx", "gy", None),
            P("gx", None, None),
            P("gx", "gy", None, None),
            P(None, "gx", "gy", None, None),
            P("gx", "gy", None, None),
        ),
        out_specs=(P(None, "gx", "gy", None), P(None, "gx", "gy", None)),
        check_vma=False,
    )
```

```python
import functools

import jax
import jax.numpy as jnp
from jax import lax
from jax.experimental import pallas as pl
from jax.experimental.pallas import tpu as pltpu
from jax.sharding import PartitionSpec as P

BLOCK = 128
ROW = 8
TURN = 5
CHUNK = 26
LATER = 4


def side_of(along):
    return 4 * (along >= ROW)


F32 = jnp.float32
BF16 = jnp.bfloat16
damping = 0.8
penalty_weight = 2.0
coarse_scale = 0.0625
stencil_weight_sum = 44.0 / 3.0
half_weight_sum = 22.0 / 3.0
MEMORY = 32 * 1024 * 1024


def iota(shape, axis):
    return lax.broadcasted_iota(jnp.int32, shape, axis)


def place():
    along = lax.axis_index("gx")
    return along, lax.axis_index("gy"), lax.rem(along, 2) == 0


def parts(value, count):
    cuts = []
    for index in range(count):
        cut = value.astype(BF16)
        cuts.append(cut)
        if index + 1 < count:
            value = value - cut.astype(F32)
    return cuts


def one_hots(cells):
    rows = cells.shape[1]
    low = iota((128, rows), 0) == (cells & 127)
    return iota((64, rows), 0) == (cells >> 7), low.astype(F32).astype(BF16)


def exact_product(value, table):
    rows = value.shape[0]
    cuts = jnp.dot(
        jnp.concatenate(parts(value, 3), axis=0), table.astype(F32).astype(BF16),
        preferred_element_type=F32,
    )
    return cuts[0:rows] + cuts[rows : 2 * rows] + cuts[2 * rows : 3 * rows]


def contract_rows(left, right):
    return lax.dot_general(left, right, (((1,), (1,)), ((), ())), preferred_element_type=F32)


def front_kernel(
    counts_in, cells_in, cond_in, rhs_in, smoothed, count, near, far, marked,
    counts, cells, cond, rhs, sems,
):
    _, own, first = place()
    pairs = ((counts_in, counts), (cells_in, cells), (cond_in, cond), (rhs_in, rhs))
    copies = [
        pltpu.make_async_copy(source, target, sems.at[i]) for i, (source, target) in enumerate(pairs)
    ]
    for copy in copies:
        copy.start()
    copies[0].wait()
    copies[1].wait()
    mine = jnp.where(iota((8, 8), 1) == own, counts[...], 0)
    limit = jnp.sum(mine, axis=1, keepdims=True) * BLOCK
    valid = jnp.where(iota((8, 256), 1) < limit, cells[...], -BLOCK)
    marked[...] = valid
    lefts, lows = [], []
    for b in range(8):
        row = valid[b : b + 1, :]
        high, low = one_hots(row)
        lefts.append(high.astype(F32).astype(BF16))
        lows.append(low)
    total = contract_rows(jnp.concatenate(lefts, axis=1), jnp.concatenate(lows, axis=1))
    count[...] = total
    copies[2].wait()
    copies[3].wait()
    field = damping * rhs[...] / (stencil_weight_sum * cond[...] + penalty_weight * total)
    smoothed[...] = field
    for f, ref in ((0, smoothed), (16, cond)):
        for grid in range(2):
            low_x = ref[grid * 32 : grid * 32 + 8, :]
            high_x = ref[grid * 32 + 24 : grid * 32 + 32, :]
            at = slice(f + grid * 8, f + grid * 8 + 8)
            near[at, :] = jnp.where(first, high_x, low_x)
            far[at, :] = jnp.where(first, low_x, high_x)


def donor_kernel(base, frac, smoothed, donors):
    field = smoothed[...]
    high = field.astype(BF16).astype(F32)
    stacked = jnp.concatenate([high, field - high, high], axis=0)
    columns = stacked.T.astype(BF16)
    q = base[...]
    grid = (q >= 2667).astype(jnp.int32)
    q = q - grid * 2667
    x = (q >= 889).astype(jnp.int32) + (q >= 1778).astype(jnp.int32)
    q = q - x * 889
    y = jnp.zeros_like(q)
    for step in range(1, 7):
        y = y + (q >= step * 127).astype(jnp.int32)
    z = q - y * 127
    plane = grid * 4 + x
    eight = iota((8, 256), 0)
    wide = iota((128, 256), 0)
    for d in range(8):
        row = slice(d, d + 1)
        frac_x, frac_y, frac_z = frac[0, row, :], frac[1, row, :], frac[2, row, :]
        at_x, at_y, at_z = plane[row], y[row], z[row]
        weight_x = jnp.where(eight == at_x, 1.0 - frac_x, jnp.where(eight == at_x + 1, frac_x, 0.0))
        weight_y = jnp.where(eight == at_y, 1.0 - frac_y, jnp.where(eight == at_y + 1, frac_y, 0.0))
        weight_z = jnp.where(wide == at_z, 1.0 - frac_z, jnp.where(wide == at_z + 1, frac_z, 0.0))
        weight = jnp.concatenate([weight_x[p : p + 1] * weight_y for p in range(8)], axis=0)
        upper, lower = parts(weight, 2)
        mixed = jnp.dot(
            columns, jnp.concatenate([upper, upper, lower], axis=0), preferred_element_type=F32
        )
        donors[row, :] = jnp.sum(mixed * weight_z, axis=0, keepdims=True)


def pack_kernel(donors, smoothed, cond, far, near, sent):
    _, own, first = place()
    faces = []
    for y in (0, 7):
        near_rows = near[pl.ds(y, 4, stride=8), :]
        far_rows = far[pl.ds(y, 4, stride=8), :]
        faces.append(
            (
                smoothed[pl.ds(y, 8, stride=8), :],
                cond[pl.ds(y, 8, stride=8), :],
                jnp.where(first, far_rows, near_rows),
                jnp.where(first, near_rows, far_rows),
            )
        )
    for d in range(8):
        start = (d - TURN) % 8 * CHUNK
        for f, (row, count) in enumerate(((0, 8), (8, 8), (16, 4), (20, 4))):
            sent[start + row : start + row + count, :] = jnp.where(
                d > own, faces[1][f], faces[0][f]
            )
        sent[start + 24 : start + 25, :] = donors[d : d + 1, 0:128]
        sent[start + 25 : start + 26, :] = donors[d : d + 1, 128:256]


def residual_kernel(
    cells, arrived, smoothed, count, rhs, cond, far, near, partial, coarse
):
    _, own, first = place()
    lefts, lows = [], []
    for b in range(8):
        high, low = one_hots(cells[b : b + 1, :])
        values = jnp.concatenate([
                arrived[(b - TURN) % 8 * CHUNK + row : (b - TURN) % 8 * CHUNK + row + 1, :]
                for row in (24, 25)
            ], axis=1)
        left = jnp.concatenate(
            [jnp.where(high, cut.astype(F32), 0.0).astype(BF16) for cut in parts(values, 2)], axis=0
        )
        lefts.append(left)
        lows.append(low)
    total = contract_rows(jnp.concatenate(lefts, axis=1), jnp.concatenate(lows, axis=1))
    total = total[0:64] + total[64:128]

    below = jnp.where(own > 0, arrived[pl.ds(((own + 7 - TURN) & 7) * CHUNK, 24), :], 0.0)
    above = jnp.where(own < 7, arrived[pl.ds(((own + 9 - TURN) & 7) * CHUNK, 24), :], 0.0)
    lanes = iota((8, 128), 1)
    rows = iota((8, 128), 0)
    keep_up = lanes < 127
    keep_down = lanes > 0

    def shift_z(value):
        return jnp.where(keep_down, pltpu.roll(value, 1, 1), 0.0) + jnp.where(
            keep_up, pltpu.roll(value, 127, 1), 0.0
        )

    def shift_y(value, lower, upper):
        down = jnp.where(rows > 0, pltpu.roll(value, 1, 0), lower)
        up = jnp.where(rows < 7, pltpu.roll(value, 7, 0), upper)
        return down + up

    pooled = []
    for grid in range(2):
        fields = []
        for f, ref in ((0, smoothed), (1, cond)):
            at = slice((2 * f + grid) * 8, (2 * f + grid) * 8 + 8)
            near_plane, far_plane = near[at, :], far[at, :]
            left = jnp.where(first, far_plane, near_plane)
            right = jnp.where(first, near_plane, far_plane)
            start = grid * 32
            planes = [left] + [ref[start + x * 8 : start + x * 8 + 8, :] for x in range(4)] + [right]
            at = [16 + 2 * f + grid] + [8 * f + grid * 4 + x for x in range(4)] + [20 + 2 * f + grid]
            lower = [below[row : row + 1, :] for row in at]
            upper = [above[row : row + 1, :] for row in at]
            fields.append((planes, lower, upper))
        fields.append(tuple([v * c for v, c in zip(*pair)] for pair in zip(*fields)))
        sums = []
        for planes, lower, upper in fields:
            inner, outer = [], []
            for plane, low_row, high_row in zip(planes, lower, upper):
                beside_z = shift_z(plane)
                beside_y = shift_y(plane, low_row, high_row)
                both = shift_z(beside_y)
                edge = beside_z + beside_y
                inner.append(0.5 * edge + 0.25 * both)
                outer.append(0.5 * plane + 0.25 * edge + (1.0 / 6.0) * both)
            sums.append([inner[i] + outer[i - 1] + outer[i + 1] for i in range(1, 5)])
        summed = jnp.zeros((8, 128), F32)
        for x in range(4):
            at = slice(grid * 32 + x * 8, grid * 32 + x * 8 + 8)
            v, c = smoothed[at, :], cond[at, :]
            applied = v * (half_weight_sum * c + sums[1][x]) - c * sums[0][x] - sums[2][x]
            value = rhs[at, :] - applied - penalty_weight * (count[at, :] * v - total[at])
            partial[at, :] = value
            summed = summed + value
        pooled.append(summed)
    for grid in range(2):
        start = grid * 32
        pooled.append(sum(cond[start + x * 8 : start + x * 8 + 8, :] for x in range(4)))

    pool = iota((128, 128), 0) // 4 == iota((128, 128), 1) % 32
    means = exact_product(jnp.concatenate(pooled, axis=0), pool) * (1.0 / 64.0)
    own_part = iota((16, 128), 0) // 4 == iota((16, 128), 1) // 32
    lines = [
        jnp.sum(jnp.where(own_part, means[f * 16 : f * 16 + 16], 0.0), axis=0, keepdims=True)
        for f in range(2)
    ]
    coarse[...] = jnp.broadcast_to(jnp.concatenate(lines, axis=0)[None], (64, 2, 128))


def pass_kernel(gathered, passed, token):
    along, own, _ = place()
    low_half = lax.rem(along, ROW) < ROW // 2
    start = ((jnp.where(low_half, ROW // 2, 0) ^ side_of(along)) & 4) + jnp.where(low_half, 1, 0)
    for r in range(5):
        line = (own + r + 6 - LATER) & 7
        passed[r * 6 : r * 6 + 6, :] = gathered[pl.ds(line * 16 + start * 2, 6), :]
    token[...] = gathered[0:8, :]


def store_kernel(token, partial, residual):
    residual[...] = partial[...]


def coarse_kernel(gathered, extra_in, smoothed, pressure, extra):
    along, own, _ = place()
    extra[...] = jnp.zeros((48, 128), F32)
    for r in range(5):
        extra[pl.ds(((own + r + 6 - LATER) & 7) * 6, 6), :] = extra_in[r * 6 : r * 6 + 6, :]
    column, side = lax.rem(along, ROW), side_of(along)
    skip = jnp.where(column < ROW // 2, 1, 0)
    lanes = iota((8, 128), 1)
    rows = (iota((8, 128), 0) + LATER) & 7
    low_z = lanes % 32 > 0
    high_z = lanes % 32 < 31
    first_y = lanes % 64 < 32

    def shift_z(value):
        return jnp.where(low_z, pltpu.roll(value, 1, 1), 0.0) + jnp.where(
            high_z, pltpu.roll(value, 127, 1), 0.0
        )

    def shift_y(value):
        ahead = pltpu.roll(value, 96, 1)
        behind = pltpu.roll(value, 32, 1)
        within = jnp.where(first_y, ahead, behind)
        from_below = jnp.where(rows > 0, pltpu.roll(ahead, 1, 0), 0.0)
        from_above = jnp.where(rows < 7, pltpu.roll(behind, 7, 0), 0.0)
        return within + jnp.where(first_y, from_below, from_above)

    def neighbour_sums(fields):
        sums = []
        for i in range(1, len(fields) - 1):
            field, beside = fields[i], fields[i - 1] + fields[i + 1]
            edge = 0.5 * field + 0.25 * beside
            corner = 0.25 * field + (1.0 / 6.0) * beside
            sums.append(0.5 * beside + shift_y(edge) + shift_z(edge + shift_y(corner)))
        return sums

    rhs, cond = [], []
    for slot in range(7):
        at = column + slot - 3
        inside = jnp.logical_and(at >= 0, at < ROW)
        here = (jnp.clip(at, 0, ROW - 1) ^ side) * 2
        there = jnp.clip((at & 3) - skip, 0, 2) * 2
        for f, out in ((0, rhs), (1, cond)):
            out.append(
                jnp.where(inside, gathered[pl.ds(here + f, 8, stride=16), :],
                    extra[pl.ds(there + f, 8, stride=6), :],)
            )
    scale = [
        jnp.where(c > 0.0, damping / (stencil_weight_sum * coarse_scale * jnp.where(c > 0.0, c, 1.0)), 0.0)
        for c in cond
    ]
    value = [r * s for r, s in zip(rhs, scale)]
    own_sum = [
        half_weight_sum * c + s for c, s in zip(cond[1:-1], neighbour_sums(cond))
    ]
    for sweep in range(3):
        around = neighbour_sums(value)
        around_both = neighbour_sums([v * c for v, c in zip(value, cond)])
        value, cond, rhs, scale = value[1:-1], cond[1:-1], rhs[1:-1], scale[1:-1]
        value = [
            v + s * (r - coarse_scale * (v * o - c * a - b))
            for v, s, r, o, c, a, b in zip(value, scale, rhs, own_sum, cond, around, around_both)
        ]
        own_sum = own_sum[1:-1]
    mine = jnp.sum(jnp.where(rows == own, value[0], 0.0), axis=0, keepdims=True)
    spread = jnp.where(iota((16, 128), 0) // 4 == iota((16, 128), 1) // 32, mine, 0.0)
    expand = iota((128, 128), 0) % 32 == iota((128, 128), 1) // 4
    fine = exact_product(spread, expand)
    for grid in range(2):
        for x in range(4):
            at = slice(grid * 32 + x * 8, grid * 32 + x * 8 + 8)
            pressure[at, :] = smoothed[at, :] + fine[grid * 8 : grid * 8 + 8]


def call(kernel, name, outs, operands, spaces, scratch=()):
    return pl.pallas_call(
        kernel,
        out_shape=[
            jax.ShapeDtypeStruct(*(out if isinstance(out[0], tuple) else (out, F32))) for out in outs
        ],
        in_specs=[pl.BlockSpec(memory_space=space) for space in spaces],
        out_specs=[pl.BlockSpec(memory_space=pltpu.VMEM)] * len(outs),
        scratch_shapes=scratch,
        compiler_params=pltpu.CompilerParams(vmem_limit_bytes=MEMORY),
        cost_estimate=pl.CostEstimate(flops=1000000, bytes_accessed=200000, transcendentals=0),
        name=name,
    )(*operands)


def local(pressure_rhs, conductivity, block_counts, donor_base, donor_frac, receptor_cells):
    shape = pressure_rhs.shape
    size = lax.axis_size("gx")
    rhs = pressure_rhs.reshape(64, 128)
    cond = conductivity.reshape(64, 128)
    counts = block_counts[0]
    cells = receptor_cells[0, 0]
    base = donor_base[0, 0]
    frac = donor_frac[:, 0, 0]
    vector, far_memory = pltpu.VMEM, pltpu.HBM
    whole = (64, 128)
    smoothed, count, near, far, marked = call(
        front_kernel, "front",
        [whole, whole, (32, 128), (32, 128), ((8, 256), jnp.int32)],
        tuple(
            pltpu.with_memory_space_constraint(value, far_memory)
            for value in (counts, cells, cond, rhs)
        ),
        [far_memory] * 4,
        [
            pltpu.VMEM((8, 8), jnp.int32),
            pltpu.VMEM((8, 256), jnp.int32),
            pltpu.VMEM(whole, F32),
            pltpu.VMEM(whole, F32),
            pltpu.SemaphoreType.DMA((4,)),
        ],
    )
    beyond = [(i, i + 1) for i in range(1, size - 1, 2)]
    far_in = lax.ppermute(far, "gx", beyond + [(j, i) for i, j in beyond])
    near_in = lax.ppermute(near, "gx", [(i, i ^ 1) for i in range(size)])
    (donors,) = call(donor_kernel, "donor", [(8, 256)], (base, frac, smoothed), [vector] * 3)
    (sent,) = call(
        pack_kernel, "pack", [(8 * CHUNK, 128)], (donors, smoothed, cond, far_in, near_in),
        [vector] * 5,
    )
    arrived = lax.all_to_all(
        sent.reshape(8 * CHUNK, 1, 128), "gy", split_axis=0, concat_axis=0, tiled=True,
        axis_index_groups=[[(i + TURN) % 8 for i in range(8)]],
    ).reshape(8 * CHUNK, 128)
    partial, coarse = call(
        residual_kernel, "residual", [whole, (64, 2, 128)],
        (marked, arrived, smoothed, count, rhs, cond, far_in, near_in), [vector] * 8,
    )
    groups = [
        [
            (start + (i ^ int(side_of(start)))) * 8 + (j + LATER) % 8
            for j in range(8)
            for i in range(ROW)
        ]
        for start in range(0, size, ROW)
    ]
    gathered = lax.all_to_all(
        coarse, ("gx", "gy"), split_axis=0, concat_axis=0, tiled=True, axis_index_groups=groups
    ).reshape(128, 128)
    passed, token = call(
        pass_kernel, "pass", [(30, 128), (8, 128)], (gathered,), [vector]
    )
    step = [(i, i + ROW) if i % ROW < ROW // 2 else (i, i - ROW) for i in range(size)]
    extra = lax.ppermute(passed, "gx", [(i, j) for i, j in step if 0 <= j < size])
    (residual,) = call(store_kernel, "store", [whole], (token, partial), [vector] * 2)
    (pressure,) = call(
        coarse_kernel, "coarse", [whole],
        (gathered, extra, smoothed), [vector] * 3, [pltpu.VMEM((48, 128), F32)],
    )
    return pressure.reshape(shape), residual.reshape(shape)


def solution(mesh):
    return jax.shard_map(
        local,
        mesh=mesh,
        in_specs=(
            P(None, "gx", "gy", None),
            P(None, "gx", "gy", None),
            P("gx", None, None),
            P("gx", "gy", None, None),
            P(None, "gx", "gy", None, None),
            P("gx", "gy", None, None),
        ),
        out_specs=(P(None, "gx", "gy", None), P(None, "gx", "gy", None)),
        check_vma=False,
    )
```
